128 devices in a mesh: dp: 16 (over z, x_lo, core), mp: 8 (over x_hi, y).
Axes of the slice: x: 4 (x_hi: 2, x_lo: 2; x = x_hi * 2 + x_lo), y: 4, z: 4, core: 2. Of those that a mesh axis runs over, the one named last changes fastest.
Arguments:
- tokens: bfloat16 [8192, 3072], P('dp', 'mp'), may hold values from -180 to 180
- update_grad: bfloat16 [8192, 3072], P('dp', 'mp'), may hold values from -1 to 1
- weight_in: bfloat16 [3072, 9216], P('dp', 'mp'), may hold values from -0.109375 to 0.109375
- weight_out: bfloat16 [3072, 3072], P('dp', 'mp'), may hold values from -0.875 to 0.875
Outputs:
- update: bfloat16 [8192, 3072], P('dp', 'mp')
- input_grad: bfloat16 [8192, 3072], P('dp', 'mp')
- weight_in_grad: float32 [3072, 9216], P('dp', 'mp')
- weight_out_grad: float32 [3072, 3072], P('dp', 'mp')
The draws below stay inside these ranges and needn't reach their ends.
All inputs are finite; a program needn't handle non-finite values.
Results may differ from the reference program's by a relative error of at most 0.023.
Values may be sent and summed in bfloat16 or wider, within the bound.
No kernel may reach another device: no remote copies, remote signals or barrier semaphores. Data moves between devices by JAX's collectives and lax.ppermute only.
A program may use at most 128 MiB of HBM per device.

```python
import math
import jax
import jax.numpy as jnp
from jax import lax

D = 3072
HEADS = 24
HD = 128
PATCH = 256
A = 3072
TOK_DEV = 512
TOKENS = 8192
IMAGES = 32
N_DP = 16


def draw_tokens(key, part):
    key = jax.random.fold_in(key, 11)
    first, second, third = jax.random.split(key, 3)
    row_scale = jnp.exp(jax.random.uniform(second, (TOKENS, 1), jnp.float32) * math.log(10.0))
    column_scale = jnp.exp(jax.random.uniform(third, (1, D), jnp.float32) * math.log(10.0))
    base = jnp.clip(jax.random.normal(first, (TOKENS, D), jnp.float32), -6.0, 6.0)
    return (0.3 * base * row_scale * column_scale).astype(jnp.bfloat16)


def strengthened(entries, rng, source, target, parts, factor):
    def block_of(position):
        return (jnp.arange(entries.shape[position]) // (entries.shape[position] // parts)).reshape((-1,) + (1,) * (entries.ndim - 1 - position))

    near = jax.random.permutation(rng, parts)[block_of(target)]
    other_side = (block_of(target) + parts // 2) % parts
    return jnp.where((block_of(source) == near) | (block_of(source) == other_side), factor * entries, entries)


def steps_of(stream_key, shape, cuts, low, top_value):
    loudness = 1.0
    for axis_at, parts in cuts:
        steps = jax.random.uniform(jax.random.fold_in(jax.random.fold_in(stream_key, 6), axis_at), (parts,), jnp.float32, low / len(cuts), top_value / len(cuts))
        loudness = loudness * jnp.repeat(jnp.exp(steps), shape[axis_at] // parts).reshape((-1,) + (1,) * (len(shape) - 1 - axis_at))
    return loudness


def gaussian(stream_key, shape, deviation, reach, shards=(), held_as=jnp.bfloat16):
    values = deviation * jax.random.normal(stream_key, shape, jnp.float32)
    if shards:
        values = values * steps_of(stream_key, shape, shards, -0.22, 0.18)
    return jnp.clip(values, -reach, reach).astype(held_as)


def bell_draw_with(stream_key, shape, deviation, bound, pieces, heavy, held_as=jnp.bfloat16):
    array = deviation * jax.random.normal(stream_key, shape, jnp.float32)
    if pieces:
        array = array * steps_of(stream_key, shape, pieces, -0.22, 0.18)
    return jnp.clip(strengthened(array, jax.random.fold_in(stream_key, 3), *heavy), -bound, bound).astype(held_as)


def setup_inputs(seed: int = 0) -> dict:
    key_list = jax.random.split(jax.random.key(seed), 5)
    return {
        "tokens": draw_tokens(jax.random.fold_in(key_list[4], 71), 0),
        "update_grad": bell_draw_with(key_list[1], (TOKENS, D), 0.05, 1.0, ((0, 16), (1, 8)), (0, 1, 16, 2.0)),
        "weight_in": gaussian(key_list[2], (D, 3 * A), D ** -0.5, 0.109375, ((0, 16), (1, 8))),
        "weight_out": gaussian(key_list[3], (D, A), (A // 64) ** -0.5, 0.875, ((0, 16), (1, 8))),
    }


epsilon = 1e-06

def norm_rows(vector):
    centred = vector - lax.optimization_barrier(jnp.mean(vector, axis=-1, keepdims=True))
    inverse = lax.rsqrt(lax.optimization_barrier(jnp.mean(centred * centred, axis=-1, keepdims=True)) + epsilon)
    return (centred * inverse, inverse)

def norm_back(incoming, normed, inverse):
    mean_in = lax.optimization_barrier(jnp.mean(incoming, axis=-1, keepdims=True))
    mean_cross = lax.optimization_barrier(jnp.mean(incoming * normed, axis=-1, keepdims=True))
    return inverse * (incoming - mean_in - normed * mean_cross)

def attend_forward(projected):
    wide = jnp.float32
    query_norm, query_scale = norm_rows(projected[:, :, :, 0])
    key_norm, key_scale = norm_rows(projected[:, :, :, 1])
    query_low = query_norm.astype(jnp.bfloat16)
    key_low = key_norm.astype(jnp.bfloat16)
    value_low = projected[:, :, :, 2].astype(jnp.bfloat16)
    query_low, key_low, value_low = lax.optimization_barrier((query_low, key_low, value_low))
    scores = jnp.einsum('bphe,bqhe->bhpq', query_low.astype(wide), key_low.astype(wide)) * HD ** (-0.5)
    expo = jnp.exp(scores)
    attention = expo / lax.optimization_barrier(jnp.sum(expo, axis=-1, keepdims=True))
    rounded = lax.optimization_barrier(attention.astype(jnp.bfloat16))
    head_out = jnp.einsum('bhpq,bqhe->bphe', rounded.astype(wide), value_low.astype(wide)).astype(jnp.bfloat16)
    saved = (attention, rounded, query_low, key_low, value_low, query_norm, query_scale, key_norm, key_scale)
    return (head_out, saved)

def attend_backward(incoming, saved):
    wide = jnp.float32
    attention, rounded, query_low, key_low, value_low, query_norm, query_scale, key_norm, key_scale = saved
    incoming = lax.optimization_barrier(incoming)
    mixing_grad = jnp.einsum('bphe,bqhe->bhpq', incoming.astype(wide), value_low.astype(wide))
    score_grad = attention * (mixing_grad - lax.optimization_barrier(jnp.sum(mixing_grad * attention, axis=-1, keepdims=True)))
    score_low = lax.optimization_barrier((score_grad * HD ** (-0.5)).astype(jnp.bfloat16))
    value_grad = jnp.einsum('bhpq,bphe->bqhe', rounded.astype(wide), incoming.astype(wide))
    query_grad = jnp.einsum('bhpq,bqhe->bphe', score_low.astype(wide), key_low.astype(wide))
    key_grad = jnp.einsum('bhpq,bphe->bqhe', score_low.astype(wide), query_low.astype(wide))
    query_grad = norm_back(query_grad, query_norm, query_scale)
    key_grad = norm_back(key_grad, key_norm, key_scale)
    return jnp.stack([query_grad, key_grad, value_grad], axis=3).astype(jnp.bfloat16)

def grouped_product(left, right):
    left_groups = left.reshape(N_DP, TOK_DEV, left.shape[1])
    right_groups = right.reshape(N_DP, TOK_DEV, right.shape[1])

    def add_group(total, pair):
        term = jnp.dot(pair[0].T, pair[1], preferred_element_type=jnp.float32)
        rounded = lax.optimization_barrier(term.astype(jnp.bfloat16))
        return (total + rounded.astype(jnp.float32), None)
    start = jnp.zeros((left.shape[1], right.shape[1]), jnp.float32)
    total, _ = lax.scan(add_group, start, (left_groups, right_groups))
    return total

def reference(tokens, update_grad, weight_in, weight_out):
    normed, inv_tokens = norm_rows(tokens.astype(jnp.float32))
    normed_low = normed.astype(jnp.bfloat16)
    projected = jnp.dot(normed_low, weight_in, preferred_element_type=jnp.float32)
    attend_grad = jnp.dot(update_grad, weight_out, preferred_element_type=jnp.float32).astype(jnp.bfloat16)
    head_out, saved = attend_forward(projected.reshape(IMAGES, PATCH, HEADS, 3, HD))
    attended = head_out.reshape(TOKENS, HEADS * HD)
    update = jnp.dot(attended, weight_out.T, preferred_element_type=jnp.float32).astype(jnp.bfloat16)
    projected_grad = attend_backward(attend_grad.reshape(IMAGES, PATCH, HEADS, HD), saved)
    projected_grad = projected_grad.reshape(TOKENS, 3 * HEADS * HD)
    weight_in_grad = grouped_product(normed_low, projected_grad)
    weight_out_grad = grouped_product(update_grad, attended)
    normed_grad = jnp.dot(projected_grad, weight_in.T, preferred_element_type=jnp.float32)
    input_grad = norm_back(normed_grad, normed, inv_tokens).astype(jnp.bfloat16)
    return (update, input_grad, weight_in_grad, weight_out_grad)
```

```python
import functools

import jax
import jax.numpy as jnp
from jax import lax
from jax.experimental import pallas as pl
from jax.experimental.pallas import tpu as pltpu
from jax.sharding import PartitionSpec as P

F32 = jnp.float32
BF16 = jnp.bfloat16

D = 3072
HD = 128
PATCH = 256
TOK = 512
HEADS = 3
WQ = HEADS * 3 * HD
WA = HEADS * HD
WALL = WQ + WA
FEAT = 384
ROWS = 192
EPS = 1e-06
EXTRA = 32
VMEM = 56 * 1024 * 1024

NN = (((1,), (0,)), ((), ()))
NT = (((1,), (1,)), ((), ()))
TN = (((0,), (0,)), ((), ()))

PIECES = ((0, 0), (0, 3), (0, 1), (0, 2), (1, 0), (1, 3), (1, 1), (1, 2))
BLOCKS = ((1, 2), (0, 2), (1, 1), (1, 3), (0, 1), (0, 3), (1, 0), (0, 0))


def dot(a, b, dims):
    return lax.dot_general(a, b, dims, preferred_element_type=F32)


def mp_perm(dx, dy):
    return [(x * 4 + y, ((x + dx) % 2) * 4 + (y + dy) % 4) for x in range(2) for y in range(4)]


def dp_perm(dz, dx, dc):
    return [
        ((z * 2 + x) * 2 + c, (((z + dz) % 4) * 2 + (x + dx) % 2) * 2 + (c + dc) % 2)
        for z in range(4)
        for x in range(2)
        for c in range(2)
    ]


def y_up(v):
    return lax.ppermute(v, "mp", mp_perm(0, 1))


def y_down(v):
    return lax.ppermute(v, "mp", mp_perm(0, 3))


def x_far(v):
    return lax.ppermute(v, "mp", mp_perm(1, 0))


def z_up(v):
    return lax.ppermute(v, "dp", dp_perm(1, 0, 0))


def z_down(v):
    return lax.ppermute(v, "dp", dp_perm(3, 0, 0))


def x_near(v):
    return lax.ppermute(v, "dp", dp_perm(0, 1, 0))


def other_core(v):
    return lax.ppermute(v, "dp", dp_perm(0, 0, 1))


def params():
    return pltpu.CompilerParams(vmem_limit_bytes=VMEM)


def cost(flops, nbytes):
    return pl.CostEstimate(flops=flops, bytes_accessed=nbytes, transcendentals=0)


def whole(shape):
    return pl.BlockSpec(shape, lambda *_: (0,) * len(shape))


def norm_rows(v):
    centred = v - jnp.mean(v, axis=-1, keepdims=True)
    inverse = lax.rsqrt(jnp.mean(centred * centred, axis=-1, keepdims=True) + EPS)
    return centred * inverse, inverse


def norm_back(incoming, normed, inverse):
    mean_in = jnp.mean(incoming, axis=-1, keepdims=True)
    mean_cross = jnp.mean(incoming * normed, axis=-1, keepdims=True)
    return inverse * (incoming - mean_in - normed * mean_cross)


PREP = 128


def prep_kernel(place, own, ap, am, fat, fag, xx, bp, bm, fbt, fbg, low, grad, low_t, grad_t, mean, inv):
    t_refs = [own.at[0], ap.at[0], am.at[0], fat, xx.at[0], bp.at[0], bm.at[0], fbt]
    g_refs = [own.at[1], ap.at[1], am.at[1], fag, xx.at[1], bp.at[1], bm.at[1], fbg]
    total = jnp.zeros((PREP, FEAT), F32)
    for r in t_refs:
        total = total + r[...].astype(F32)
    m = jnp.sum(total, axis=-1, keepdims=True) * (1.0 / D)
    total = jnp.zeros((PREP, FEAT), F32)
    for r in t_refs:
        c = r[...].astype(F32) - m
        total = total + c * c
    i = lax.rsqrt(jnp.sum(total, axis=-1, keepdims=True) * (1.0 / D) + EPS)
    mean[...] = m
    inv[...] = i
    for k in range(8):
        at = pl.multiple_of(place[k] * FEAT, FEAT)
        n = ((t_refs[k][...].astype(F32) - m) * i).astype(BF16)
        low[:, pl.ds(at, FEAT)] = n
        low_t[pl.ds(at, FEAT), :] = n.T
        g = g_refs[k][...]
        grad[:, pl.ds(at, FEAT)] = g
        grad_t[pl.ds(at, FEAT), :] = g.T


def prep(place, pieces):
    pair = pl.BlockSpec((2, PREP, FEAT), lambda i, s: (0, i, 0))
    one = pl.BlockSpec((PREP, FEAT), lambda i, s: (i, 0))
    row = pl.BlockSpec((PREP, D), lambda i, s: (i, 0))
    col = pl.BlockSpec((D, PREP), lambda i, s: (0, i))
    stat = pl.BlockSpec((PREP, 1), lambda i, s: (i, 0))
    return pl.pallas_call(
        prep_kernel,
        grid_spec=pltpu.PrefetchScalarGridSpec(
            num_scalar_prefetch=1,
            grid=(TOK // PREP,),
            in_specs=[pair, pair, pair, one, one, pair, pair, pair, one, one],
            out_specs=[row, row, col, col, stat, stat],
        ),
        out_shape=[
            jax.ShapeDtypeStruct((TOK, D), BF16),
            jax.ShapeDtypeStruct((TOK, D), BF16),
            jax.ShapeDtypeStruct((D, TOK), BF16),
            jax.ShapeDtypeStruct((D, TOK), BF16),
            jax.ShapeDtypeStruct((TOK, 1), F32),
            jax.ShapeDtypeStruct((TOK, 1), F32),
        ],
        compiler_params=params(),
        cost_estimate=cost(20 * TOK * D, 6 * TOK * D * 2),
        name="prep",
    )(place, *pieces)


def eye():
    return lax.broadcasted_iota(jnp.int32, (HD, HD), 0) == lax.broadcasted_iota(jnp.int32, (HD, HD), 1)


def attend_kernel(low, grad, w, attended, dproj, stats, acc, gacc, wsum, rows):
    k = pl.program_id(0)

    @pl.when(k == 0)
    def _():
        acc[...] = jnp.zeros_like(acc)
        gacc[...] = jnp.zeros_like(gacc)
        wsum[...] = jnp.zeros_like(wsum)
        rows[...] = jnp.zeros_like(rows)

    acc[...] += dot(low[...], w[:, :WQ], NN)
    gacc[...] += dot(grad[...], w[:, WQ:], NN)
    wsum[...] += jnp.sum(w[:, :WQ].astype(F32), axis=0, keepdims=True)

    @pl.when(k == 7)
    def _():
        scale = HD**-0.5
        for b in range(TOK // PATCH):
            at = slice(b * PATCH, (b + 1) * PATCH)
            sum_in = jnp.zeros((PATCH, HD), F32)
            sum_cross = jnp.zeros((PATCH, HD), F32)
            for h in range(HEADS):
                c = h * 3 * HD
                parts = [slice(c + p * HD, c + (p + 1) * HD) for p in range(3)]
                q, key, v = [acc[at, s] for s in parts]
                qn, qs = norm_rows(q)
                kn, ks = norm_rows(key)
                ql, kl, vl = qn.astype(BF16), kn.astype(BF16), v.astype(BF16)
                expo = jnp.exp(dot(ql, kl, NT) * scale)
                att = expo / jnp.sum(expo, axis=-1, keepdims=True)
                att_low = att.astype(BF16)
                hs = slice(h * HD, (h + 1) * HD)
                attended[at, hs] = dot(att_low, vl, NN).astype(BF16)
                g = gacc[at, hs].astype(BF16)
                mix = dot(g, vl, NT)
                sg = att * (mix - jnp.sum(mix * att, axis=-1, keepdims=True))
                sg = (sg * scale).astype(BF16)
                dv = dot(att_low, g, TN)
                dq = norm_back(dot(sg, kl, NN), qn, qs)
                dk = norm_back(dot(sg, ql, TN), kn, ks)
                for s, d, value in zip(parts, (dq, dk, dv), (q, key, v)):
                    d = d.astype(BF16)
                    dproj[at, s] = d
                    d = d.astype(F32)
                    sum_in = sum_in + d * wsum[:, s]
                    sum_cross = sum_cross + d * value
            s_in = jnp.sum(sum_in, axis=-1, keepdims=True)
            s_cross = jnp.sum(sum_cross, axis=-1, keepdims=True)
            for t in range(PATCH // HD):
                r = b * (PATCH // HD) + t
                part = slice(t * HD, (t + 1) * HD)
                rows[r : r + 1, :HD] = jnp.sum(jnp.where(eye(), s_in[part], 0.0), axis=0, keepdims=True)
                rows[r + 4 : r + 5, :HD] = jnp.sum(jnp.where(eye(), s_cross[part], 0.0), axis=0, keepdims=True)
        stats[...] = rows[...].astype(BF16)


def attend(low, grad, w):
    return pl.pallas_call(
        attend_kernel,
        grid=(8,),
        in_specs=[
            pl.BlockSpec((TOK, FEAT), lambda k: (0, k)),
            pl.BlockSpec((TOK, FEAT), lambda k: (0, k)),
            pl.BlockSpec((FEAT, WALL), lambda k: (k, 0)),
        ],
        out_specs=[whole((TOK, WA)), whole((TOK, WQ)), whole((EXTRA, FEAT))],
        out_shape=[
            jax.ShapeDtypeStruct((TOK, WA), BF16),
            jax.ShapeDtypeStruct((TOK, WQ), BF16),
            jax.ShapeDtypeStruct((EXTRA, FEAT), BF16),
        ],
        scratch_shapes=[
            pltpu.VMEM((TOK, WQ), F32),
            pltpu.VMEM((TOK, WA), F32),
            pltpu.VMEM((1, WQ), F32),
            pltpu.VMEM((EXTRA, FEAT), F32),
        ],
        compiler_params=pltpu.CompilerParams(vmem_limit_bytes=VMEM),
        cost_estimate=cost(2 * TOK * D * WALL + 8 * 2 * TOK * PATCH * WA, 16 * 1024 * 1024),
        name="attend",
    )(low, grad, w)


def store_steps(j, block, half, s_up, s_down, mids, lasts):
    for far in range(2):

        @pl.when(j == far)
        def _(far=far):
            s_up[far] = block[:half]
            s_down[far] = block[half:]

    for i, ref in enumerate(mids):

        @pl.when(j == 2 + i)
        def _(ref=ref):
            ref[...] = block

    for i, ref in enumerate(lasts):

        @pl.when(j == 6 + i)
        def _(ref=ref):
            ref[...] = block


def step_shapes(rows, width):
    half = [(2, rows // 2, width)] * 2
    return half + [(rows, width)] * 6


def token_kernel(with_stats, place, left, w, *refs):
    j = pl.program_id(0)
    outs = refs[1:] if with_stats else refs
    block = dot(left[...], w[...], NT).astype(BF16)
    if with_stats:
        block = jnp.concatenate([block, refs[0][...]], axis=0)
    store_steps(j, block, block.shape[0] // 2, outs[0], outs[1], outs[2:6], outs[6:8])


def token_blocks(place, left, w, column, stats=None):
    width = left.shape[1]
    rows = TOK + (EXTRA if stats is not None else 0)
    shapes = step_shapes(rows, FEAT)
    ins = [left, w] + ([stats] if stats is not None else [])
    return pl.pallas_call(
        functools.partial(token_kernel, stats is not None),
        grid_spec=pltpu.PrefetchScalarGridSpec(
            num_scalar_prefetch=1,
            grid=(8,),
            in_specs=[
                whole((TOK, width)),
                pl.BlockSpec((FEAT, width), lambda j, s: (s[j], column)),
            ]
            + ([whole((EXTRA, FEAT))] if stats is not None else []),
            out_specs=[whole(s) for s in shapes],
        ),
        out_shape=[jax.ShapeDtypeStruct(s, BF16) for s in shapes],
        compiler_params=params(),
        cost_estimate=cost(2 * TOK * D * width, (D * width + TOK * width + rows * D) * 2),
        name="token_blocks",
    )(place, *ins)


def weight_send_kernel(place, low_t, grad_t, dproj, attended, out):
    out[0, :, :WQ] = dot(low_t[...], dproj[...], NN).astype(BF16)
    out[0, :, WQ:] = dot(grad_t[...], attended[...], NN).astype(BF16)


def weight_keep_kernel(place, low_t, grad_t, dproj, attended, came, *outs):
    j = pl.program_id(0)
    other = came[0].astype(F32)
    block = jnp.concatenate(
        [
            (dot(low_t[...], dproj[...], NN) + other[:, :WQ]).astype(BF16),
            (dot(grad_t[...], attended[...], NN) + other[:, WQ:]).astype(BF16),
        ],
        axis=1,
    )
    store_steps(j, block, ROWS // 2, outs[0], outs[1], outs[2:6], outs[6:8])


def weight_blocks(place, low_t, grad_t, dproj, attended, came=None):
    strip = pl.BlockSpec((ROWS, TOK), lambda j, s: (s[j], 0))
    block = pl.BlockSpec((1, ROWS, WALL), lambda j, s: (j, 0, 0))
    in_specs = [strip, strip, whole((TOK, WQ)), whole((TOK, WA))]
    if came is None:
        shapes = [(8, ROWS, WALL)]
        kernel, out_specs, ins = weight_send_kernel, [block], ()
    else:
        shapes = step_shapes(ROWS, WALL)
        in_specs = in_specs + [block]
        kernel, out_specs, ins = weight_keep_kernel, [whole(s) for s in shapes], (came,)
    return pl.pallas_call(
        kernel,
        grid_spec=pltpu.PrefetchScalarGridSpec(
            num_scalar_prefetch=1, grid=(8,), in_specs=in_specs, out_specs=out_specs
        ),
        out_shape=[jax.ShapeDtypeStruct(s, BF16) for s in shapes],
        compiler_params=params(),
        cost_estimate=cost(TOK * D * WALL, 3 * D * WALL),
        name="weight_blocks",
    )(place, low_t, grad_t, dproj, attended, *ins)


def plus(*values):
    return functools.reduce(lambda a, b: a + b, [v.astype(F32) for v in values]).astype(BF16)


def reduce_ring(blocks, up, down, across):
    s_up, s_down, a1, a3, b1, b3, a0, b0 = blocks
    half = s_up.shape[1]
    from_up, from_down = up(s_up), down(s_down)
    a1 = a1.at[:half].set(plus(a1[:half], from_up[0]))
    a3 = a3.at[half:].set(plus(a3[half:], from_down[0]))
    ra, rb = up(a1), down(a3)
    b1 = b1.at[:half].set(plus(b1[:half], from_up[1]))
    b3 = b3.at[half:].set(plus(b3[half:], from_down[1]))
    rc, rd = up(b1), down(b3)
    rx = across(plus(a0, ra, rb))
    return b0, rc, rd, rx


def grads_kernel(a, b, c, d, out_in, out_out):
    total = a[...].astype(F32) + b[...].astype(F32) + c[...].astype(F32) + d[...].astype(F32)
    out_in[...] = total[:, :WQ]
    out_out[...] = total[:, WQ:]


def last_grads(parts):
    return pl.pallas_call(
        grads_kernel,
        out_shape=[jax.ShapeDtypeStruct((ROWS, WQ), F32), jax.ShapeDtypeStruct((ROWS, WA), F32)],
        compiler_params=params(),
        cost_estimate=cost(4 * ROWS * WALL, 12 * ROWS * WALL),
        name="last_grads",
    )(*parts)


def input_kernel(a, b, c, d, tokens, mean, inv, out):
    total = a[TOK:].astype(F32) + b[TOK:].astype(F32) + c[TOK:].astype(F32) + d[TOK:].astype(F32)
    for g in range(TOK // HD):
        at = slice(g * HD, (g + 1) * HD)
        value = a[at].astype(F32) + b[at].astype(F32) + c[at].astype(F32) + d[at].astype(F32)
        m_in = jnp.sum(jnp.where(eye(), total[g : g + 1, :HD], 0.0), axis=1, keepdims=True) * (1.0 / D)
        m_cross = jnp.sum(jnp.where(eye(), total[g + 4 : g + 5, :HD], 0.0), axis=1, keepdims=True) * (1.0 / D)
        i = inv[at]
        normed = (tokens[at].astype(F32) - mean[at]) * i
        out[at] = (i * (value - m_in - normed * m_cross)).astype(BF16)


def last_input(parts, tokens, mean, inv):
    return pl.pallas_call(
        input_kernel,
        out_shape=jax.ShapeDtypeStruct((TOK, FEAT), BF16),
        compiler_params=params(),
        cost_estimate=cost(12 * TOK * FEAT, 12 * TOK * FEAT),
        name="last_input",
    )(*parts, tokens, mean, inv)


def local(tokens, update_grad, weight_in, weight_out):
    m = lax.axis_index("mp")
    x, y = m // 4, m % 4
    d = lax.axis_index("dp")
    z, near, core = d // 4, (d // 2) % 2, d % 2
    place_in = jnp.stack([((x + a) % 2) * 4 + (y + b) % 4 for a, b in PIECES]).astype(jnp.int32)
    place_tok = jnp.stack([((x + a) % 2) * 4 + (y + b) % 4 for a, b in BLOCKS]).astype(jnp.int32)
    strips = [((z + b) % 4) * 4 + ((near + a) % 2) * 2 for a, b in BLOCKS]
    place_keep = jnp.stack([s + core for s in strips]).astype(jnp.int32)
    place_send = jnp.stack([s + 1 - core for s in strips]).astype(jnp.int32)

    w = lax.all_gather(jnp.concatenate([weight_in, weight_out], axis=1), "dp", axis=0, tiled=True)

    own = jnp.stack([tokens, update_grad])
    ap, am = y_up(own), y_down(own)
    xx = x_far(own)
    bp, bm = y_up(xx), y_down(xx)
    fat, fag = y_up(ap[0]), y_down(am[1])
    fbt, fbg = y_up(bp[0]), y_down(bm[1])

    low, grad, low_t, grad_t, mean, inv = prep(place_in, (own, ap, am, fat, fag, xx, bp, bm, fbt, fbg))
    attended, dproj, stats = attend(low, grad, w)

    update_parts = reduce_ring(token_blocks(place_tok, attended, w, 3), y_up, y_down, x_far)
    update = plus(*update_parts)

    (send,) = weight_blocks(place_send, low_t, grad_t, dproj, attended)
    came = other_core(send)
    normed_blocks = token_blocks(place_tok, dproj, w, 0, stats)
    keep = weight_blocks(place_keep, low_t, grad_t, dproj, attended, came)
    grad_parts = reduce_ring(keep, z_up, z_down, x_near)
    input_parts = reduce_ring(normed_blocks, y_up, y_down, x_far)
    weight_in_grad, weight_out_grad = last_grads(grad_parts)
    input_grad = last_input(input_parts, tokens, mean, inv)
    return (update, input_grad, weight_in_grad, weight_out_grad)


def solution(mesh):
    return jax.shard_map(
        local,
        mesh=mesh,
        in_specs=(P("dp", "mp"), P("dp", "mp"), P("dp", "mp"), P("dp", "mp")),
        out_specs=(P("dp", "mp"), P("dp", "mp"), P("dp", "mp"), P("dp", "mp")),
        check_vma=False,
    )
```

```python
import functools

import jax
import jax.numpy as jnp
from jax import lax
from jax.experimental import pallas as pl
from jax.experimental.pallas import tpu as pltpu
from jax.sharding import PartitionSpec as P

F32 = jnp.float32
BF16 = jnp.bfloat16

D = 3072
HD = 128
PATCH = 256
TOK = 512
HEADS = 3
WQ = HEADS * 3 * HD
WA = HEADS * HD
WALL = WQ + WA
FEAT = 384
ROWS = 192
EPS = 1e-06
EXTRA = 32

NN = (((1,), (0,)), ((), ()))
NT = (((1,), (1,)), ((), ()))
TN = (((0,), (0,)), ((), ()))

PIECES = ((0, 0), (0, 3), (0, 1), (0, 2), (1, 0), (1, 3), (1, 1), (1, 2))
BLOCKS = ((1, 2), (0, 2), (1, 1), (1, 3), (0, 1), (0, 3), (1, 0), (0, 0))


def dot(a, b, dims):
    return lax.dot_general(a, b, dims, preferred_element_type=F32)


def mp_perm(dx, dy):
    return [(x * 4 + y, ((x + dx) % 2) * 4 + (y + dy) % 4) for x in range(2) for y in range(4)]


def dp_perm(dz, dx, dc):
    return [
        ((z * 2 + x) * 2 + c, (((z + dz) % 4) * 2 + (x + dx) % 2) * 2 + (c + dc) % 2)
        for z in range(4)
        for x in range(2)
        for c in range(2)
    ]


def y_up(v):
    return lax.ppermute(v, "mp", mp_perm(0, 1))


def y_down(v):
    return lax.ppermute(v, "mp", mp_perm(0, 3))


def x_far(v):
    return lax.ppermute(v, "mp", mp_perm(1, 0))


def z_up(v):
    return lax.ppermute(v, "dp", dp_perm(1, 0, 0))


def z_down(v):
    return lax.ppermute(v, "dp", dp_perm(3, 0, 0))


def x_near(v):
    return lax.ppermute(v, "dp", dp_perm(0, 1, 0))


def other_core(v):
    return lax.ppermute(v, "dp", dp_perm(0, 0, 1))


IN_HBM = pl.BlockSpec(memory_space=pltpu.HBM)
IN_VMEM = pl.BlockSpec(memory_space=pltpu.VMEM)


def in_hbm(values):
    return [pltpu.with_memory_space_constraint(v, pltpu.HBM) for v in values]


def call(kernel, name, mib, ins, outs, scratch, flops, args):
    return pl.pallas_call(
        kernel,
        in_specs=ins,
        out_specs=[o for o, _ in outs],
        out_shape=[s for _, s in outs],
        scratch_shapes=scratch,
        compiler_params=pltpu.CompilerParams(vmem_limit_bytes=mib * 1024 * 1024),
        cost_estimate=pl.CostEstimate(flops=flops, bytes_accessed=8 * 1024 * 1024, transcendentals=0),
        name=name,
    )(*args)


def to_vmem(shape, dtype=BF16):
    return IN_VMEM, pltpu.VMEM(shape, dtype)


def either(shape, dtype=BF16):
    return IN_VMEM, jax.ShapeDtypeStruct(shape, dtype)


def after(value, *others):
    return lax.optimization_barrier((value, others))[0]


def norm_rows(v):
    centred = v - jnp.mean(v, axis=-1, keepdims=True)
    inverse = lax.rsqrt(jnp.mean(centred * centred, axis=-1, keepdims=True) + EPS)
    return centred * inverse, inverse


def norm_back(incoming, normed, inverse):
    mean_in = jnp.mean(incoming, axis=-1, keepdims=True)
    mean_cross = jnp.mean(incoming * normed, axis=-1, keepdims=True)
    return inverse * (incoming - mean_in - normed * mean_cross)


PIECE_SHAPES = [(TOK, FEAT)] * 6 + [(2, TOK // 2, FEAT)] * 2


def piece_of(refs, k, at, rows):
    own, ap, am, xx, bp, bm, f0, f1 = refs
    if k == 3 or k == 7:
        half = TOK // 2
        return (f0 if at < half else f1)[k // 4, at % half : at % half + rows, :]
    return (own, ap, am, None, xx, bp, bm)[k][at : at + rows, :]


def columns_of(orders, k):
    m = lax.axis_index("mp")
    far, step = orders[k]
    owner = ((m // 4 + far) % 2) * 4 + (m + step) % 4
    return pl.ds(pl.multiple_of(owner * FEAT, FEAT), FEAT)


def strip_of(k, other):
    d = lax.axis_index("dp")
    far, step = BLOCKS[k]
    owner = ((d // 4 + step) % 4) * 4 + (((d // 2) + far) % 2) * 2 + (d + other) % 2
    return pl.ds(pl.multiple_of(owner * ROWS, ROWS), ROWS)


def tokens_kernel(*refs):
    held, (low, low_t, mean, inv) = refs[:8], refs[8:12]
    for at in range(0, TOK, HD):
        rows = slice(at, at + HD)
        total = jnp.zeros((HD, FEAT), F32)
        for k in range(8):
            total = total + piece_of(held, k, at, HD).astype(F32)
        m = jnp.sum(total, axis=-1, keepdims=True) * (1.0 / D)
        total = jnp.zeros((HD, FEAT), F32)
        for k in range(8):
            c = piece_of(held, k, at, HD).astype(F32) - m
            total = total + c * c
        i = lax.rsqrt(jnp.sum(total, axis=-1, keepdims=True) * (1.0 / D) + EPS)
        mean[rows, :] = m
        inv[rows, :] = i
        for k in range(8):
            to = columns_of(PIECES, k)
            n = ((piece_of(held, k, at, HD).astype(F32) - m) * i).astype(BF16)
            low[rows, to] = n
            low_t[to, rows] = n.T


def grad_kernel(*refs):
    held, (grad, grad_t) = refs[:8], refs[8:10]
    half = TOK // 2
    for k in range(8):
        to = columns_of(PIECES, k)
        for at in (0, half):
            v = piece_of(held, k, at, half)
            grad[at : at + half, to] = v
            grad_t[to, at : at + half] = v.T


def tokens_in_order(pieces):
    outs = [either((TOK, D)), either((D, TOK)), either((TOK, 1), F32), either((TOK, 1), F32)]
    return call(tokens_kernel, "tokens", 8, [IN_VMEM] * 8, outs, [], 20 * TOK * D, pieces)


def grad_in_order(pieces):
    outs = [either((TOK, D)), either((D, TOK))]
    return call(grad_kernel, "cotangent", 8, [IN_VMEM] * 8, outs, [], 2 * TOK * D, pieces)


CHUNKS = 4


def attend_kernel(low, grad, w, attended, dproj, dproj_t, wv, *refs):
    outs = refs[:8]
    acc, sems = refs[8:]
    depth = D // CHUNKS
    loads = []
    for k in range(CHUNKS):
        at = pl.ds(k * depth, depth)
        loads.append(pltpu.make_async_copy(w.at[at, :], wv.at[at, :], sems.at[k]))
        loads[k].start()
    for k in range(CHUNKS):
        loads[k].wait()
        at = slice(k * depth, (k + 1) * depth)
        first = dot(low[:, at], wv[at, :WQ], NN)
        second = dot(grad[:, at], wv[at, WQ:], NN)
        if k == 0:
            acc[:, :WQ] = first
            acc[:, WQ:] = second
        else:
            acc[:, :WQ] += first
            acc[:, WQ:] += second

    scale = HD**-0.5
    units = [(b, h) for b in range(TOK // PATCH) for h in range(HEADS)]

    def part(u, p):
        b, h = u
        c = WQ + h * HD if p == 3 else (h * 3 + p) * HD
        return acc[b * PATCH : (b + 1) * PATCH, c : c + HD]

    def keep(u, p, value):
        b, h = u
        c = (h * 3 + p) * HD
        value = value.astype(BF16)
        dproj[b * PATCH : (b + 1) * PATCH, c : c + HD] = value
        dproj_t[c : c + HD, b * PATCH : (b + 1) * PATCH] = value.T

    queries = [norm_rows(part(u, 0)) for u in units]
    keys = [norm_rows(part(u, 1)) for u in units]
    ql = [v[0].astype(BF16) for v in queries]
    kl = [v[0].astype(BF16) for v in keys]
    vl = [part(u, 2).astype(BF16) for u in units]
    gl = [part(u, 3).astype(BF16) for u in units]
    scores = [dot(a, b, NT) * scale for a, b in zip(ql, kl)]
    mixes = [dot(g, v, NT) for g, v in zip(gl, vl)]
    expo = [jnp.exp(v) for v in scores]
    att = [v / jnp.sum(v, axis=-1, keepdims=True) for v in expo]
    att_low = [v.astype(BF16) for v in att]
    mixed = [dot(a, v, NN).astype(BF16) for a, v in zip(att_low, vl)]
    sg = [a * (m - jnp.sum(m * a, axis=-1, keepdims=True)) for a, m in zip(att, mixes)]
    sg = [(v * scale).astype(BF16) for v in sg]
    for (b, h), v in zip(units, mixed):
        attended[b * PATCH : (b + 1) * PATCH, h * HD : (h + 1) * HD] = v
    for u, a, g in zip(units, att_low, gl):
        keep(u, 2, dot(a, g, TN))
    for u, v, k, q in zip(units, sg, kl, queries):
        keep(u, 0, norm_back(dot(v, k, NN), *q))
    for u, v, q, k in zip(units, sg, ql, keys):
        keep(u, 1, norm_back(dot(v, q, TN), *k))

    attended_t = attended[...].T
    for j in range(8):
        store_step(j, dot(wv[columns_of(BLOCKS, j), WQ:], attended_t, NN).astype(BF16), outs)


def attend(low, grad, w):
    outs = [either((TOK, WA)), either((TOK, WQ)), either((WQ, TOK)), to_vmem((D, WALL))]
    outs += [either(s) for s in step_shapes(FEAT, TOK)]
    scratch = [pltpu.VMEM((TOK, WALL), F32), pltpu.SemaphoreType.DMA((CHUNKS,))]
    flops = 2 * TOK * D * (WALL + WA) + 8 * 2 * TOK * PATCH * WA
    args = (low, grad, *in_hbm((w,)))
    out = call(attend_kernel, "attend", 20, [IN_VMEM, IN_VMEM, IN_HBM], outs, scratch, flops, args)
    return out[:4], out[4:]


def store_step(j, block, outs):
    half = block.shape[0] // 2
    if j < 2:
        outs[0][j] = block[:half]
        outs[1][j] = block[half:]
    else:
        outs[j][...] = block


def step_shapes(rows, width):
    return [(2, rows // 2, width)] * 2 + [(rows, width)] * 6


def normed_kernel(dproj_t, low_t, w, *outs):
    half = (FEAT + EXTRA) // 2
    s_in = jnp.zeros((1, TOK), F32)
    s_cross = jnp.zeros((1, TOK), F32)
    for j in range(8):
        at = columns_of(BLOCKS, j)
        block = dot(w[at, :WQ], dproj_t[...], NN)
        s_in = s_in + jnp.sum(block, axis=0, keepdims=True)
        s_cross = s_cross + jnp.sum(block * low_t[at, :].astype(F32), axis=0, keepdims=True)
        block = block.astype(BF16)
        if j < 2:
            outs[0][j] = block[:half]
            outs[1][j, : FEAT - half] = block[half:]
        else:
            outs[j][:FEAT] = block
    stats = jnp.concatenate([s_in, s_cross, jnp.zeros((EXTRA - 2, TOK), F32)], axis=0).astype(BF16)
    for j in range(8):
        if j < 2:
            outs[1][j, FEAT - half :] = stats
        else:
            outs[j][FEAT:] = stats


def normed_blocks(dproj_t, low_t, w):
    outs = [either(s) for s in step_shapes(FEAT + EXTRA, TOK)]
    return call(normed_kernel, "normed_blocks", 8, [IN_VMEM] * 3, outs, [], 2 * TOK * D * WQ, (dproj_t, low_t, w))


def weight_send_kernel(low_t, grad_t, dproj, attended, out):
    for j in range(8):
        at = strip_of(j, 1)
        out[j, :, :WQ] = dot(low_t[at, :], dproj[...], NN).astype(BF16)
        out[j, :, WQ:] = dot(grad_t[at, :], attended[...], NN).astype(BF16)


def weight_keep_kernel(low_t, grad_t, dproj, attended, came, *outs):
    for j in range(8):
        at = strip_of(j, 0)
        first = dot(low_t[at, :], dproj[...], NN) + came[j, :, :WQ].astype(F32)
        second = dot(grad_t[at, :], attended[...], NN) + came[j, :, WQ:].astype(F32)
        store_step(j, jnp.concatenate([first.astype(BF16), second.astype(BF16)], axis=1), outs)


def weight_blocks(low_t, grad_t, dproj, attended, came=None):
    args = (low_t, grad_t, dproj, attended)
    if came is None:
        kernel, name, outs = weight_send_kernel, "weight_send", [either((8, ROWS, WALL))]
    else:
        kernel, name, outs = weight_keep_kernel, "weight_keep", [either(s) for s in step_shapes(ROWS, WALL)]
        args = args + (came,)
    return call(kernel, name, 8, [IN_VMEM] * len(args), outs, [], TOK * D * WALL, args)


def plus(*values):
    return functools.reduce(lambda a, b: a + b, [v.astype(F32) for v in values]).astype(BF16)


def grads_kernel(a, b, c, d, out_in, out_out):
    total = a[...].astype(F32) + b[...].astype(F32) + c[...].astype(F32) + d[...].astype(F32)
    out_in[...] = total[:, :WQ]
    out_out[...] = total[:, WQ:]


def last_grads(parts):
    outs = [either((ROWS, WQ), F32), either((ROWS, WA), F32)]
    return call(grads_kernel, "last_grads", 8, [IN_VMEM] * 4, outs, [], 4 * ROWS * WALL, parts)


def update_kernel(a, b, c, d, out):
    total = a[...].astype(F32) + b[...].astype(F32) + c[...].astype(F32) + d[...].astype(F32)
    out[...] = total.T.astype(BF16)


def last_update(parts):
    return call(update_kernel, "last_update", 8, [IN_VMEM] * 4, [either((TOK, FEAT))], [], TOK * FEAT, parts)[0]


def input_kernel(a, b, c, d, tokens, mean, inv, out):
    total = a[...].astype(F32) + b[...].astype(F32) + c[...].astype(F32) + d[...].astype(F32)
    value = (total[:FEAT] - total[FEAT : FEAT + 1] * (1.0 / D)).T
    cross = jnp.broadcast_to(total[FEAT + 1 : FEAT + 2] * (1.0 / D), (8, TOK)).T[:, :1]
    i = inv[...]
    normed = (tokens[...].astype(F32) - mean[...]) * i
    out[...] = (i * (value - normed * cross)).astype(BF16)


def last_input(parts, tokens, mean, inv):
    args = (*parts, tokens, mean, inv)
    return call(input_kernel, "last_input", 8, [IN_VMEM] * 7, [either((TOK, FEAT))], [], TOK * FEAT, args)[0]


def local(tokens, update_grad, weight_in, weight_out):
    w = lax.all_gather(jnp.concatenate([weight_in, weight_out], axis=1), "dp", axis=0, tiled=True)

    half = TOK // 2
    t_ap, t_am, t_xx = y_up(tokens), y_down(tokens), x_far(tokens)
    g_ap, g_am, g_xx = y_up(update_grad), y_down(update_grad), x_far(update_grad)
    t_bp, t_bm = y_up(t_xx), y_down(t_xx)
    t_f0 = y_up(jnp.stack([t_ap[:half], t_bp[:half]]))
    t_f1 = y_down(jnp.stack([t_am[half:], t_bm[half:]]))
    g_xx = after(g_xx, t_bp, t_bm)
    g_bp, g_bm = y_up(g_xx), y_down(g_xx)
    g_f0 = y_up(jnp.stack([g_ap[:half], g_bp[:half]]))
    g_f1 = y_down(jnp.stack([g_am[half:], g_bm[half:]]))
    low, low_t, mean, inv = tokens_in_order((tokens, t_ap, t_am, t_xx, t_bp, t_bm, t_f0, t_f1))
    grad, grad_t = grad_in_order((update_grad, g_ap, g_am, g_xx, g_bp, g_bm, g_f0, g_f1))

    (attended, dproj, dproj_t, w), u = attend(low, grad, w)

    u_up, u_down = y_up(u[0]), y_down(u[1])
    (send,) = weight_blocks(low_t, grad_t, dproj, attended)
    came = other_core(send)
    n = normed_blocks(after(dproj_t, send), low_t, w)

    h = FEAT // 2
    u_up, u_down = after((u_up, u_down), n[7])
    u_s1 = jnp.stack([u[2].at[:h].set(plus(u[2][:h], u_up[0])), u[4].at[:h].set(plus(u[4][:h], u_up[1]))])
    u_s3 = jnp.stack([u[3].at[h:].set(plus(u[3][h:], u_down[0])), u[5].at[h:].set(plus(u[5][h:], u_down[1]))])
    u_r1, u_r3 = y_up(u_s1), y_down(u_s3)

    keep = weight_blocks(low_t, grad_t, dproj, attended, after(came, u_s1, u_s3))
    k_up, k_down = z_up(keep[0]), z_down(keep[1])

    u_r1, u_r3 = after((u_r1, u_r3), keep[7])
    u_x = x_far(plus(u[6], u_r1[0], u_r3[0]))
    n_first = after((n[0], n[1]), u_r1, u_r3)
    n_up, n_down = y_up(n_first[0]), y_down(n_first[1])

    r = ROWS // 2
    k_up, k_down = after((k_up, k_down), *n_first)
    k_a = [keep[2].at[:r].set(plus(keep[2][:r], k_up[0])), keep[3].at[r:].set(plus(keep[3][r:], k_down[0]))]
    k_r = z_up(k_a[0]), z_down(k_a[1])

    q = (FEAT + EXTRA) // 2
    n_up, n_down = after((n_up, n_down), *k_a)
    n_a = [n[2].at[:q].set(plus(n[2][:q], n_up[0])), n[3].at[q:].set(plus(n[3][q:], n_down[0]))]
    n_r = y_up(n_a[0]), y_down(n_a[1])

    k_r, k_up, k_down = after((k_r, k_up, k_down), *n_a)
    k_b = [keep[4].at[:r].set(plus(keep[4][:r], k_up[1])), keep[5].at[r:].set(plus(keep[5][r:], k_down[1]))]
    k_b = after(k_b, *k_r)
    k_x = x_near(plus(keep[6], *k_r))
    k_q = z_up(k_b[0]), z_down(k_b[1])

    n_r, n_up, n_down = after((n_r, n_up, n_down), *k_b)
    n_b = [n[4].at[:q].set(plus(n[4][:q], n_up[1])), n[5].at[q:].set(plus(n[5][q:], n_down[1]))]
    n_b = after(n_b, *n_r)
    n_x = x_far(plus(n[6], *n_r))
    n_q = y_up(n_b[0]), y_down(n_b[1])

    u_x = after(u_x, *n_b)
    update = last_update((u[7], u_r1[1], u_r3[1], u_x))
    input_grad = last_input((n[7], *n_q, n_x), tokens, mean, inv)
    weight_in_grad, weight_out_grad = last_grads((keep[7], *k_q, k_x))
    return (update, input_grad, weight_in_grad, weight_out_grad)


def solution(mesh):
    return jax.shard_map(
        local,
        mesh=mesh,
        in_specs=(P("dp", "mp"), P("dp", "mp"), P("dp", "mp"), P("dp", "mp")),
        out_specs=(P("dp", "mp"), P("dp", "mp"), P("dp", "mp"), P("dp", "mp")),
        check_vma=False,
    )
```

```python
import functools

import jax
import jax.numpy as jnp
from jax import lax
from jax.experimental import pallas as pl
from jax.experimental.pallas import tpu as pltpu
from jax.sharding import PartitionSpec as P

F32 = jnp.float32
BF16 = jnp.bfloat16

D = 3072
HD = 128
PATCH = 256
TOK = 512
HEADS = 3
WQ = HEADS * 3 * HD
WA = HEADS * HD
WALL = WQ + WA
FEAT = 384
ROWS = 192
EPS = 1e-06
EXTRA = 32

NN = (((1,), (0,)), ((), ()))
NT = (((1,), (1,)), ((), ()))
TN = (((0,), (0,)), ((), ()))

PIECES = ((0, 0), (0, 3), (0, 1), (0, 2), (1, 0), (1, 3), (1, 1), (1, 2))
BLOCKS = ((1, 2), (0, 2), (1, 1), (1, 3), (0, 1), (0, 3), (1, 0), (0, 0))


def dot(a, b, dims):
    return lax.dot_general(a, b, dims, preferred_element_type=F32)


def mp_perm(dx, dy):
    return [(x * 4 + y, ((x + dx) % 2) * 4 + (y + dy) % 4) for x in range(2) for y in range(4)]


def dp_perm(dz, dx, dc):
    return [
        ((z * 2 + x) * 2 + c, (((z + dz) % 4) * 2 + (x + dx) % 2) * 2 + (c + dc) % 2)
        for z in range(4)
        for x in range(2)
        for c in range(2)
    ]


def y_up(v):
    return lax.ppermute(v, "mp", mp_perm(0, 1))


def y_down(v):
    return lax.ppermute(v, "mp", mp_perm(0, 3))


def x_far(v):
    return lax.ppermute(v, "mp", mp_perm(1, 0))


def z_up(v):
    return lax.ppermute(v, "dp", dp_perm(1, 0, 0))


def z_down(v):
    return lax.ppermute(v, "dp", dp_perm(3, 0, 0))


def x_near(v):
    return lax.ppermute(v, "dp", dp_perm(0, 1, 0))


def other_core(v):
    return lax.ppermute(v, "dp", dp_perm(0, 0, 1))


IN_HBM = pl.BlockSpec(memory_space=pltpu.HBM)
IN_VMEM = pl.BlockSpec(memory_space=pltpu.VMEM)


def in_hbm(values):
    return [pltpu.with_memory_space_constraint(v, pltpu.HBM) for v in values]


def call(kernel, name, mib, ins, outs, scratch, flops, args):
    return pl.pallas_call(
        kernel,
        in_specs=ins,
        out_specs=[o for o, _ in outs],
        out_shape=[s for _, s in outs],
        scratch_shapes=scratch,
        compiler_params=pltpu.CompilerParams(vmem_limit_bytes=mib * 1024 * 1024),
        cost_estimate=pl.CostEstimate(flops=1024, bytes_accessed=1024, transcendentals=0),
        name=name,
    )(*args)


def to_vmem(shape, dtype=BF16):
    return IN_VMEM, pltpu.VMEM(shape, dtype)


def either(shape, dtype=BF16):
    return IN_VMEM, jax.ShapeDtypeStruct(shape, dtype)


def after(value, *others):
    return lax.optimization_barrier((value, others))[0]


def norm_rows(v):
    centred = v - jnp.mean(v, axis=-1, keepdims=True)
    inverse = lax.rsqrt(jnp.mean(centred * centred, axis=-1, keepdims=True) + EPS)
    return centred * inverse, inverse


def norm_back(incoming, normed, inverse):
    mean_in = jnp.mean(incoming, axis=-1, keepdims=True)
    mean_cross = jnp.mean(incoming * normed, axis=-1, keepdims=True)
    return inverse * (incoming - mean_in - normed * mean_cross)


PIECE_SHAPES = [(TOK, FEAT)] * 6 + [(2, TOK // 2, FEAT)] * 2


def piece_of(refs, k, at, rows):
    own, ap, am, xx, bp, bm, f0, f1 = refs
    if k == 3 or k == 7:
        half = TOK // 2
        return (f0 if at < half else f1)[k // 4, at % half : at % half + rows, :]
    return (own, ap, am, None, xx, bp, bm)[k][at : at + rows, :]


def columns_of(orders, k):
    m = lax.axis_index("mp")
    far, step = orders[k]
    owner = ((m // 4 + far) % 2) * 4 + (m + step) % 4
    return pl.ds(pl.multiple_of(owner * FEAT, FEAT), FEAT)


def strip_of(k, other):
    d = lax.axis_index("dp")
    far, step = BLOCKS[k]
    owner = ((d // 4 + step) % 4) * 4 + (((d // 2) + far) % 2) * 2 + (d + other) % 2
    return pl.ds(pl.multiple_of(owner * ROWS, ROWS), ROWS)


def tokens_kernel(*refs):
    held, (low, low_t, mean, inv) = refs[:8], refs[8:12]
    for at in range(0, TOK, HD):
        rows = slice(at, at + HD)
        total = jnp.zeros((HD, FEAT), F32)
        for k in range(8):
            total = total + piece_of(held, k, at, HD).astype(F32)
        m = jnp.sum(total, axis=-1, keepdims=True) * (1.0 / D)
        total = jnp.zeros((HD, FEAT), F32)
        for k in range(8):
            c = piece_of(held, k, at, HD).astype(F32) - m
            total = total + c * c
        i = lax.rsqrt(jnp.sum(total, axis=-1, keepdims=True) * (1.0 / D) + EPS)
        mean[rows, :] = m
        inv[rows, :] = i
        for k in range(8):
            to = columns_of(PIECES, k)
            n = ((piece_of(held, k, at, HD).astype(F32) - m) * i).astype(BF16)
            low[rows, to] = n
            low_t[to, rows] = n.T


def grad_kernel(*refs):
    held, (grad, grad_t) = refs[:8], refs[8:10]
    half = TOK // 2
    for k in range(8):
        to = columns_of(PIECES, k)
        for at in (0, half):
            v = piece_of(held, k, at, half)
            grad[at : at + half, to] = v
            grad_t[to, at : at + half] = v.T


def tokens_in_order(pieces):
    outs = [either((TOK, D)), either((D, TOK)), either((TOK, 1), F32), either((TOK, 1), F32)]
    return call(tokens_kernel, "tokens", 8, [IN_VMEM] * 8, outs, [], 20 * TOK * D, pieces)


def grad_in_order(pieces):
    outs = [either((TOK, D)), either((D, TOK))]
    return call(grad_kernel, "cotangent", 8, [IN_VMEM] * 8, outs, [], 2 * TOK * D, pieces)


def rows_kernel(own, near, up, down, f0, f1, result, out, sem):
    d = lax.axis_index("dp")
    half = ROWS // 2
    for far in range(2):
        for step in range(4):
            at = ((d // 4 + step) % 4) * 2 + ((d // 2) + far) % 2
            if step == 0:
                out[at] = (own, near)[far][...]
            elif step == 3:
                out[at] = up[far]
            elif step == 1:
                out[at] = down[far]
            else:
                out[at, :half] = f0[far]
                out[at, half:] = f1[far]
    copy = pltpu.make_async_copy(out, result, sem)
    copy.start()
    copy.wait()


def rows_in_order(pieces):
    outs = [(IN_HBM, pltpu.HBM((8, ROWS, WA), BF16))]
    scratch = [pltpu.VMEM((8, ROWS, WA), BF16), pltpu.SemaphoreType.DMA]
    return call(rows_kernel, "rows", 4, [IN_VMEM] * 6, outs, scratch, TOK, pieces)[0]


CHUNKS = 4
SCALE = HD**-0.5
UNITS = [(b, h) for b in range(TOK // PATCH) for h in range(HEADS)]


def head_part(ref, unit, p):
    b, h = unit
    c = (h * 3 + p) * HD
    return ref[b * PATCH : (b + 1) * PATCH, c : c + HD]


def attend_kernel(low, w, mine, others, attended, proj, att, wv, wo, *refs):
    outs = refs[:8]
    low_v, sems = refs[8:]
    depth = D // CHUNKS
    loads = []
    for k in range(CHUNKS):
        at = pl.ds(k * depth, depth)
        pair = (
            pltpu.make_async_copy(w.at[at, :], wv.at[at, :], sems.at[k]),
            pltpu.make_async_copy(low.at[:, at], low_v.at[:, at], sems.at[CHUNKS + k]),
        )
        for c in pair:
            c.start()
        loads.append(pair)
    core = lax.axis_index("dp") % 2
    rows = []
    for j in range(8):
        for half, ref in ((core, mine), (1 - core, others)):
            at = pl.ds(pl.multiple_of(j * 2 * ROWS + half * ROWS, ROWS), ROWS)
            rows.append(pltpu.make_async_copy(ref.at[j], wo.at[at, :], sems.at[2 * CHUNKS + len(rows)]))
            rows[-1].start()
    for k in range(CHUNKS):
        for c in loads[k]:
            c.wait()
        at = slice(k * depth, (k + 1) * depth)
        term = dot(low_v[:, at], wv[at, :], NN)
        if k == 0:
            proj[...] = term
        else:
            proj[...] += term
    ql = [norm_rows(head_part(proj, u, 0))[0].astype(BF16) for u in UNITS]
    kl = [norm_rows(head_part(proj, u, 1))[0].astype(BF16) for u in UNITS]
    vl = [head_part(proj, u, 2).astype(BF16) for u in UNITS]
    expo = [jnp.exp(dot(a, b, NT) * SCALE) for a, b in zip(ql, kl)]
    full = [v / jnp.sum(v, axis=-1, keepdims=True) for v in expo]
    mixed = [dot(a.astype(BF16), v, NN).astype(BF16) for a, v in zip(full, vl)]
    for i, (b, h) in enumerate(UNITS):
        att[i] = full[i]
        attended[b * PATCH : (b + 1) * PATCH, h * HD : (h + 1) * HD] = mixed[i]
    attended_t = attended[...].T
    for c in rows:
        c.wait()
    for j in range(8):
        store_step(j, dot(wo[columns_of(BLOCKS, j), :], attended_t, NN).astype(BF16), outs)


def attend(low, w, mine, others):
    outs = [either((TOK, WA)), to_vmem((TOK, WQ), F32), to_vmem((len(UNITS), PATCH, PATCH), F32)]
    outs += [to_vmem((D, WQ)), to_vmem((D, WA))]
    outs += [either(s) for s in step_shapes(FEAT, TOK)]
    scratch = [pltpu.VMEM((TOK, D), BF16), pltpu.SemaphoreType.DMA((2 * CHUNKS + 16,))]
    flops = 2 * TOK * D * WALL + 4 * TOK * PATCH * WA
    args = in_hbm((low, w, mine, others))
    out = call(attend_kernel, "attend", 16, [IN_HBM] * 4, outs, scratch, flops, args)
    return out[:5], out[5:]


def back_kernel(grad, wo, proj, att, dproj, dproj_t):
    ag = dot(grad[...], wo[...], NN).astype(BF16)

    def keep(unit, p, value):
        b, h = unit
        c = (h * 3 + p) * HD
        value = value.astype(BF16)
        dproj[b * PATCH : (b + 1) * PATCH, c : c + HD] = value
        dproj_t[c : c + HD, b * PATCH : (b + 1) * PATCH] = value.T

    queries = [norm_rows(head_part(proj, u, 0)) for u in UNITS]
    keys = [norm_rows(head_part(proj, u, 1)) for u in UNITS]
    ql = [v[0].astype(BF16) for v in queries]
    kl = [v[0].astype(BF16) for v in keys]
    vl = [head_part(proj, u, 2).astype(BF16) for u in UNITS]
    gl = [ag[b * PATCH : (b + 1) * PATCH, h * HD : (h + 1) * HD] for b, h in UNITS]
    mixes = [dot(g, v, NT) for g, v in zip(gl, vl)]
    sg = [att[i] * (m - jnp.sum(m * att[i], axis=-1, keepdims=True)) for i, m in enumerate(mixes)]
    sg = [(v * SCALE).astype(BF16) for v in sg]
    for i, u in enumerate(UNITS):
        keep(u, 2, dot(att[i].astype(BF16), gl[i], TN))
    for u, v, k, q in zip(UNITS, sg, kl, queries):
        keep(u, 0, norm_back(dot(v, k, NN), *q))
    for u, v, q, k in zip(UNITS, sg, ql, keys):
        keep(u, 1, norm_back(dot(v, q, TN), *k))


def attend_back(grad, wo, proj, att):
    outs = [either((TOK, WQ)), either((WQ, TOK))]
    flops = 2 * TOK * D * WA + 8 * TOK * PATCH * WA
    return call(back_kernel, "attend_back", 16, [IN_VMEM] * 4, outs, [], flops, (grad, wo, proj, att))


def store_step(j, block, outs):
    half = block.shape[0] // 2
    if j < 2:
        outs[0][j] = block[:half]
        outs[1][j] = block[half:]
    else:
        outs[j][...] = block


def step_shapes(rows, width):
    return [(2, rows // 2, width)] * 2 + [(rows, width)] * 6


def normed_kernel(dproj_t, low_t, w, *outs):
    half = (FEAT + EXTRA) // 2
    s_in = jnp.zeros((1, TOK), F32)
    s_cross = jnp.zeros((1, TOK), F32)
    for j in range(8):
        at = columns_of(BLOCKS, j)
        block = dot(w[at, :], dproj_t[...], NN)
        s_in = s_in + jnp.sum(block, axis=0, keepdims=True)
        s_cross = s_cross + jnp.sum(block * low_t[at, :].astype(F32), axis=0, keepdims=True)
        block = block.astype(BF16)
        if j < 2:
            outs[0][j] = block[:half]
            outs[1][j, : FEAT - half] = block[half:]
        else:
            outs[j][:FEAT] = block
    stats = jnp.concatenate([s_in, s_cross, jnp.zeros((EXTRA - 2, TOK), F32)], axis=0).astype(BF16)
    for j in range(8):
        if j < 2:
            outs[1][j, FEAT - half :] = stats
        else:
            outs[j][FEAT:] = stats


def normed_blocks(dproj_t, low_t, w):
    outs = [either(s) for s in step_shapes(FEAT + EXTRA, TOK)]
    return call(normed_kernel, "normed_blocks", 8, [IN_VMEM] * 3, outs, [], 2 * TOK * D * WQ, (dproj_t, low_t, w))


def weight_send_kernel(low_t, grad_t, dproj, attended, out):
    for j in range(8):
        at = strip_of(j, 1)
        out[j, :, :WQ] = dot(low_t[at, :], dproj[...], NN).astype(BF16)
        out[j, :, WQ:] = dot(grad_t[at, :], attended[...], NN).astype(BF16)


def weight_keep_kernel(low_t, grad_t, dproj, attended, came, *outs):
    for j in range(8):
        at = strip_of(j, 0)
        first = dot(low_t[at, :], dproj[...], NN) + came[j, :, :WQ].astype(F32)
        second = dot(grad_t[at, :], attended[...], NN) + came[j, :, WQ:].astype(F32)
        store_step(j, jnp.concatenate([first.astype(BF16), second.astype(BF16)], axis=1), outs)


def weight_blocks(low_t, grad_t, dproj, attended, came=None):
    args = (low_t, grad_t, dproj, attended)
    if came is None:
        kernel, name, outs = weight_send_kernel, "weight_send", [either((8, ROWS, WALL))]
    else:
        kernel, name, outs = weight_keep_kernel, "weight_keep", [either(s) for s in step_shapes(ROWS, WALL)]
        args = args + (came,)
    return call(kernel, name, 8, [IN_VMEM] * len(args), outs, [], TOK * D * WALL, args)


def plus(*values):
    return functools.reduce(lambda a, b: a + b, [v.astype(F32) for v in values]).astype(BF16)


def grads_kernel(a, b, c, d, out_in, out_out):
    total = a[...].astype(F32) + b[...].astype(F32) + c[...].astype(F32) + d[...].astype(F32)
    out_in[...] = total[:, :WQ]
    out_out[...] = total[:, WQ:]


def last_grads(parts):
    outs = [either((ROWS, WQ), F32), either((ROWS, WA), F32)]
    return call(grads_kernel, "last_grads", 8, [IN_VMEM] * 4, outs, [], 4 * ROWS * WALL, parts)


def update_kernel(a, b, c, d, out):
    total = a[...].astype(F32) + b[...].astype(F32) + c[...].astype(F32) + d[...].astype(F32)
    out[...] = total.T.astype(BF16)


def last_update(parts):
    return call(update_kernel, "last_update", 8, [IN_VMEM] * 4, [either((TOK, FEAT))], [], TOK * FEAT, parts)[0]


def input_kernel(a, b, c, d, tokens, mean, inv, out):
    total = a[...].astype(F32) + b[...].astype(F32) + c[...].astype(F32) + d[...].astype(F32)
    value = (total[:FEAT] - total[FEAT : FEAT + 1] * (1.0 / D)).T
    cross = jnp.broadcast_to(total[FEAT + 1 : FEAT + 2] * (1.0 / D), (8, TOK)).T[:, :1]
    i = inv[...]
    normed = (tokens[...].astype(F32) - mean[...]) * i
    out[...] = (i * (value - normed * cross)).astype(BF16)


def last_input(parts, tokens, mean, inv):
    args = (*parts, tokens, mean, inv)
    return call(input_kernel, "last_input", 8, [IN_VMEM] * 7, [either((TOK, FEAT))], [], TOK * FEAT, args)[0]


def local(tokens, update_grad, weight_in, weight_out):
    w = lax.all_gather(weight_in, "dp", axis=0, tiled=True)

    half, r = TOK // 2, ROWS // 2
    t_ap, t_am, t_xx = y_up(tokens), y_down(tokens), x_far(tokens)
    o_xx = x_near(weight_out)
    g_xx = x_far(update_grad)
    g_own = after(update_grad, t_ap, t_am)
    g_ap, g_am = y_up(g_own), y_down(g_own)
    t_bp, t_bm = y_up(t_xx), y_down(t_xx)

    o_pair = jnp.stack([weight_out, after(o_xx, t_xx, g_ap)])
    o_up, o_down = z_up(o_pair), z_down(o_pair)

    t_bp, t_bm = after((t_bp, t_bm), o_pair)
    t_s0, t_s1 = jnp.stack([t_ap[:half], t_bp[:half]]), jnp.stack([t_am[half:], t_bm[half:]])
    t_f0, t_f1 = y_up(t_s0), y_down(t_s1)
    g_xx = after(g_xx, t_s0, t_s1)
    g_bp, g_bm = y_up(g_xx), y_down(g_xx)
    o_up, o_down = after((o_up, o_down), g_xx)
    o_s0, o_s1 = o_up[:, :r], o_down[:, r:]
    o_f0, o_f1 = z_up(o_s0), z_down(o_s1)

    t_f0, t_f1 = after((t_f0, t_f1), o_s0, o_s1)
    low, low_t, mean, inv = tokens_in_order((tokens, t_ap, t_am, t_xx, t_bp, t_bm, t_f0, t_f1))
    mine = rows_in_order((weight_out, o_xx, o_up, o_down, *after((o_f0, o_f1), mean)))
    others = other_core(mine)
    g_bp, g_bm = after((g_bp, g_bm), mine)
    g_f0 = y_up(jnp.stack([g_ap[:half], g_bp[:half]]))
    g_f1 = y_down(jnp.stack([g_am[half:], g_bm[half:]]))

    (attended, proj, att, w, wo), u = attend(low, w, mine, others)
    g_f0, g_f1 = after((g_f0, g_f1), attended)
    grad, grad_t = grad_in_order((update_grad, g_ap, g_am, g_xx, g_bp, g_bm, g_f0, g_f1))

    u_up, u_down = y_up(u[0]), y_down(u[1])
    dproj, dproj_t = attend_back(grad, wo, proj, att)
    (send,) = weight_blocks(low_t, grad_t, dproj, attended)
    u_up, u_down = after((u_up, u_down), send)
    came = other_core(after(send, u_up, u_down))

    h = FEAT // 2
    u_s1 = jnp.stack([u[2].at[:h].set(plus(u[2][:h], u_up[0])), u[4].at[:h].set(plus(u[4][:h], u_up[1]))])
    u_s3 = jnp.stack([u[3].at[h:].set(plus(u[3][h:], u_down[0])), u[5].at[h:].set(plus(u[5][h:], u_down[1]))])
    u_r1, u_r3 = y_up(u_s1), y_down(u_s3)

    n = normed_blocks(after(dproj_t, u_s1, u_s3), low_t, w)
    keep = weight_blocks(low_t, grad_t, dproj, attended, after(came, n[7]))
    k_up, k_down = z_up(keep[0]), z_down(keep[1])

    u_r1, u_r3 = after((u_r1, u_r3), keep[7])
    u_x = x_far(plus(u[6], u_r1[0], u_r3[0]))
    n_first = after(n[1], u_r1, u_r3)
    n_up, n_down = y_up(after(n[0], keep[7])), y_down(n_first)

    k_up, k_down = after((k_up, k_down), n_first)
    k_a = [keep[2].at[:r].set(plus(keep[2][:r], k_up[0])), keep[3].at[r:].set(plus(keep[3][r:], k_down[0]))]
    k_r = z_up(k_a[0]), z_down(k_a[1])

    q = (FEAT + EXTRA) // 2
    n_up, n_down = after((n_up, n_down), *k_a)
    n_a = [n[2].at[:q].set(plus(n[2][:q], n_up[0])), n[3].at[q:].set(plus(n[3][q:], n_down[0]))]
    n_r = y_up(n_a[0]), y_down(n_a[1])
    n_b = [n[4].at[:q].set(plus(n[4][:q], n_up[1])), n[5].at[q:].set(plus(n[5][q:], n_down[1]))]
    n_b[0] = after(n_b[0], u_x, *n_a)
    n_q_up = y_up(n_b[0])

    k_r, k_up, k_down = after((k_r, k_up, k_down), n_b[0])
    k_b = [keep[4].at[:r].set(plus(keep[4][:r], k_up[1])), keep[5].at[r:].set(plus(keep[5][r:], k_down[1]))]
    k_b = after(k_b, *k_r)
    k_x = x_near(plus(keep[6], *k_r))
    k_q = z_up(k_b[0]), z_down(k_b[1])

    n_r = after(n_r, *k_b)
    n_q_down = y_down(after(n_b[1], n_q_up, *n_r))
    n_x = x_far(plus(n[6], *n_r))
    n_q = n_q_up, n_q_down

    update = last_update((u[7], u_r1[1], u_r3[1], u_x))
    weight_in_grad, weight_out_grad = last_grads((keep[7], *k_q, k_x))
    n_q, n_x = after((n_q, n_x), weight_in_grad)
    input_grad = last_input((n[7], *n_q, n_x), tokens, mean, inv)
    return (update, input_grad, weight_in_grad, weight_out_grad)


def solution(mesh):
    return jax.shard_map(
        local,
        mesh=mesh,
        in_specs=(P("dp", "mp"), P("dp", "mp"), P("dp", "mp"), P("dp", "mp")),
        out_specs=(P("dp", "mp"), P("dp", "mp"), P("dp", "mp"), P("dp", "mp")),
        check_vma=False,
    )
```

```python
import functools

import jax
import jax.numpy as jnp
from jax import lax
from jax.experimental import pallas as pl
from jax.experimental.pallas import tpu as pltpu
from jax.sharding import PartitionSpec as P

F32 = jnp.float32
BF16 = jnp.bfloat16

D = 3072
HD = 128
PATCH = 256
TOK = 512
HEADS = 3
WQ = HEADS * 3 * HD
WA = HEADS * HD
WALL = WQ + WA
FEAT = 384
ROWS = 192
EPS = 1e-06
EXTRA = 32

NN = (((1,), (0,)), ((), ()))
NT = (((1,), (1,)), ((), ()))
TN = (((0,), (0,)), ((), ()))

PIECES = ((0, 0), (0, 3), (0, 1), (0, 2), (1, 0), (1, 3), (1, 1), (1, 2))
BLOCKS = ((1, 2), (0, 2), (1, 1), (1, 3), (0, 1), (0, 3), (1, 0), (0, 0))


def dot(a, b, dims):
    return lax.dot_general(a, b, dims, preferred_element_type=F32)


def mp_perm(dx, dy):
    return [(x * 4 + y, ((x + dx) % 2) * 4 + (y + dy) % 4) for x in range(2) for y in range(4)]


def dp_perm(dz, dx, dc):
    return [
        ((z * 2 + x) * 2 + c, (((z + dz) % 4) * 2 + (x + dx) % 2) * 2 + (c + dc) % 2)
        for z in range(4)
        for x in range(2)
        for c in range(2)
    ]


def y_up(v):
    return lax.ppermute(v, "mp", mp_perm(0, 1))


def y_down(v):
    return lax.ppermute(v, "mp", mp_perm(0, 3))


def x_far(v):
    return lax.ppermute(v, "mp", mp_perm(1, 0))


def z_up(v):
    return lax.ppermute(v, "dp", dp_perm(1, 0, 0))


def z_down(v):
    return lax.ppermute(v, "dp", dp_perm(3, 0, 0))


def x_near(v):
    return lax.ppermute(v, "dp", dp_perm(0, 1, 0))


def other_core(v):
    return lax.ppermute(v, "dp", dp_perm(0, 0, 1))


IN_HBM = pl.BlockSpec(memory_space=pltpu.HBM)
IN_VMEM = pl.BlockSpec(memory_space=pltpu.VMEM)


def in_hbm(values):
    return [pltpu.with_memory_space_constraint(v, pltpu.HBM) for v in values]


def call(kernel, name, mib, ins, outs, scratch, flops, args):
    return pl.pallas_call(
        kernel,
        in_specs=ins,
        out_specs=[o for o, _ in outs],
        out_shape=[s for _, s in outs],
        scratch_shapes=scratch,
        compiler_params=pltpu.CompilerParams(vmem_limit_bytes=mib * 1024 * 1024),
        cost_estimate=pl.CostEstimate(flops=1024, bytes_accessed=1024, transcendentals=0),
        name=name,
    )(*args)


def to_vmem(shape, dtype=BF16):
    return IN_VMEM, pltpu.VMEM(shape, dtype)


def either(shape, dtype=BF16):
    return IN_VMEM, jax.ShapeDtypeStruct(shape, dtype)


def after(value, *others):
    return lax.optimization_barrier((value, others))[0]


def norm_rows(v):
    centred = v - jnp.mean(v, axis=-1, keepdims=True)
    inverse = lax.rsqrt(jnp.mean(centred * centred, axis=-1, keepdims=True) + EPS)
    return centred * inverse, inverse


def norm_back(incoming, normed, inverse):
    mean_in = jnp.mean(incoming, axis=-1, keepdims=True)
    mean_cross = jnp.mean(incoming * normed, axis=-1, keepdims=True)
    return inverse * (incoming - mean_in - normed * mean_cross)


PIECE_SHAPES = [(TOK, FEAT)] * 6 + [(2, TOK // 2, FEAT)] * 2


def piece_of(refs, k, at, rows):
    own, ap, am, xx, bp, bm, f0, f1 = refs
    if k == 3 or k == 7:
        half = TOK // 2
        return (f0 if at < half else f1)[k // 4, at % half : at % half + rows, :]
    return (own, ap, am, None, xx, bp, bm)[k][at : at + rows, :]


def columns_of(orders, k):
    m = lax.axis_index("mp")
    far, step = orders[k]
    owner = ((m // 4 + far) % 2) * 4 + (m + step) % 4
    return pl.ds(pl.multiple_of(owner * FEAT, FEAT), FEAT)


def strip_of(k, other):
    d = lax.axis_index("dp")
    far, step = BLOCKS[k]
    owner = ((d // 4 + step) % 4) * 4 + (((d // 2) + far) % 2) * 2 + (d + other) % 2
    return pl.ds(pl.multiple_of(owner * ROWS, ROWS), ROWS)


def tokens_kernel(*refs):
    held, (low, low_t, mean, inv) = refs[:8], refs[8:12]
    for at in range(0, TOK, HD):
        rows = slice(at, at + HD)
        total = jnp.zeros((HD, FEAT), F32)
        for k in range(8):
            total = total + piece_of(held, k, at, HD).astype(F32)
        m = jnp.sum(total, axis=-1, keepdims=True) * (1.0 / D)
        total = jnp.zeros((HD, FEAT), F32)
        for k in range(8):
            c = piece_of(held, k, at, HD).astype(F32) - m
            total = total + c * c
        i = lax.rsqrt(jnp.sum(total, axis=-1, keepdims=True) * (1.0 / D) + EPS)
        mean[rows, :] = m
        inv[rows, :] = i
        for k in range(8):
            to = columns_of(PIECES, k)
            n = ((piece_of(held, k, at, HD).astype(F32) - m) * i).astype(BF16)
            low[rows, to] = n
            low_t[to, rows] = n.T


def grad_kernel(*refs):
    held, (grad, grad_t) = refs[:8], refs[8:10]
    half = TOK // 2
    for k in range(8):
        to = columns_of(PIECES, k)
        for at in (0, half):
            v = piece_of(held, k, at, half)
            grad[at : at + half, to] = v
            grad_t[to, at : at + half] = v.T


def tokens_in_order(pieces):
    outs = [either((TOK, D)), either((D, TOK)), either((TOK, 1), F32), either((TOK, 1), F32)]
    return call(tokens_kernel, "tokens", 8, [IN_VMEM] * 8, outs, [], 20 * TOK * D, pieces)


def grad_in_order(pieces):
    outs = [either((TOK, D)), either((D, TOK))]
    return call(grad_kernel, "cotangent", 8, [IN_VMEM] * 8, outs, [], 2 * TOK * D, pieces)


def rows_kernel(own, near, up, down, near_up, near_down, f0, f1, out):
    d = lax.axis_index("dp")
    half = ROWS // 2
    for far in range(2):
        for step in range(4):
            at = ((d // 4 + step) % 4) * 2 + ((d // 2) + far) % 2
            if step == 2:
                out[at, :half] = f0[far]
                out[at, half:] = f1[far]
            else:
                pieces = ((own, down, None, up), (near, near_down, None, near_up))
                out[at] = pieces[far][step][...]


def rows_in_order(pieces):
    return call(rows_kernel, "rows", 4, [IN_VMEM] * 8, [either((8, ROWS, WALL))], [], TOK, pieces)[0]


SCALE = HD**-0.5
UNITS = [(b, h) for b in range(TOK // PATCH) for h in range(HEADS)]


def head_part(ref, unit, p):
    b, h = unit
    c = (h * 3 + p) * HD
    return ref[b * PATCH : (b + 1) * PATCH, c : c + HD]


def attend_kernel(low, mine, others, attended, proj, att, w, *outs):
    core = lax.axis_index("dp") % 2
    for k in range(4):
        for j in (2 * k, 2 * k + 1):
            w[pl.ds(pl.multiple_of(j * 2 * ROWS + core * ROWS, ROWS), ROWS), :] = mine[j]
            w[pl.ds(pl.multiple_of(j * 2 * ROWS + (1 - core) * ROWS, ROWS), ROWS), :] = others[j]
        at = slice(k * 4 * ROWS, (k + 1) * 4 * ROWS)
        term = dot(low[:, at], w[at, :WQ], NN)
        if k == 0:
            proj[...] = term
        else:
            proj[...] += term
    ql = [norm_rows(head_part(proj, u, 0))[0].astype(BF16) for u in UNITS]
    kl = [norm_rows(head_part(proj, u, 1))[0].astype(BF16) for u in UNITS]
    vl = [head_part(proj, u, 2).astype(BF16) for u in UNITS]
    expo = [jnp.exp(dot(a, b, NT) * SCALE) for a, b in zip(ql, kl)]
    full = [v / jnp.sum(v, axis=-1, keepdims=True) for v in expo]
    mixed = [dot(a.astype(BF16), v, NN).astype(BF16) for a, v in zip(full, vl)]
    for i, (b, h) in enumerate(UNITS):
        att[i] = full[i]
        attended[b * PATCH : (b + 1) * PATCH, h * HD : (h + 1) * HD] = mixed[i]
    attended_t = attended[...].T
    for j in range(8):
        store_step(j, dot(w[columns_of(BLOCKS, j), WQ:], attended_t, NN).astype(BF16), outs)


def attend(low, mine, others):
    outs = [either((TOK, WA)), to_vmem((TOK, WQ), F32), to_vmem((len(UNITS), PATCH, PATCH), F32), to_vmem((D, WALL))]
    outs += [either(s) for s in step_shapes(FEAT, TOK)]
    flops = 2 * TOK * D * WALL + 4 * TOK * PATCH * WA
    out = call(attend_kernel, "attend", 12, [IN_VMEM] * 3, outs, [], flops, (low, mine, others))
    return out[:4], out[4:]


def back_kernel(grad, w, proj, att, dproj, dproj_t):
    ag = dot(grad[...], w[:, WQ:], NN).astype(BF16)

    def keep(unit, p, value):
        b, h = unit
        c = (h * 3 + p) * HD
        value = value.astype(BF16)
        dproj[b * PATCH : (b + 1) * PATCH, c : c + HD] = value
        dproj_t[c : c + HD, b * PATCH : (b + 1) * PATCH] = value.T

    queries = [norm_rows(head_part(proj, u, 0)) for u in UNITS]
    keys = [norm_rows(head_part(proj, u, 1)) for u in UNITS]
    ql = [v[0].astype(BF16) for v in queries]
    kl = [v[0].astype(BF16) for v in keys]
    vl = [head_part(proj, u, 2).astype(BF16) for u in UNITS]
    gl = [ag[b * PATCH : (b + 1) * PATCH, h * HD : (h + 1) * HD] for b, h in UNITS]
    mixes = [dot(g, v, NT) for g, v in zip(gl, vl)]
    sg = [att[i] * (m - jnp.sum(m * att[i], axis=-1, keepdims=True)) for i, m in enumerate(mixes)]
    sg = [(v * SCALE).astype(BF16) for v in sg]
    for i, u in enumerate(UNITS):
        keep(u, 2, dot(att[i].astype(BF16), gl[i], TN))
    for u, v, k, q in zip(UNITS, sg, kl, queries):
        keep(u, 0, norm_back(dot(v, k, NN), *q))
    for u, v, q, k in zip(UNITS, sg, ql, keys):
        keep(u, 1, norm_back(dot(v, q, TN), *k))


def attend_back(grad, w, proj, att):
    outs = [either((TOK, WQ)), either((WQ, TOK))]
    flops = 2 * TOK * D * WA + 8 * TOK * PATCH * WA
    return call(back_kernel, "attend_back", 16, [IN_VMEM] * 4, outs, [], flops, (grad, w, proj, att))


def store_step(j, block, outs):
    half = block.shape[0] // 2
    if j < 2:
        outs[0][j] = block[:half]
        outs[1][j] = block[half:]
    else:
        outs[j][...] = block


def step_shapes(rows, width):
    return [(2, rows // 2, width)] * 2 + [(rows, width)] * 6


def normed_kernel(dproj_t, low_t, w, *outs):
    half = (FEAT + EXTRA) // 2
    s_in = jnp.zeros((1, TOK), F32)
    s_cross = jnp.zeros((1, TOK), F32)
    for j in range(8):
        at = columns_of(BLOCKS, j)
        block = dot(w[at, :WQ], dproj_t[...], NN)
        s_in = s_in + jnp.sum(block, axis=0, keepdims=True)
        s_cross = s_cross + jnp.sum(block * low_t[at, :].astype(F32), axis=0, keepdims=True)
        block = block.astype(BF16)
        if j < 2:
            outs[0][j] = block[:half]
            outs[1][j, : FEAT - half] = block[half:]
        else:
            outs[j][:FEAT] = block
    stats = jnp.concatenate([s_in, s_cross, jnp.zeros((EXTRA - 2, TOK), F32)], axis=0).astype(BF16)
    for j in range(8):
        if j < 2:
            outs[1][j, FEAT - half :] = stats
        else:
            outs[j][FEAT:] = stats


def normed_blocks(dproj_t, low_t, w):
    outs = [either(s) for s in step_shapes(FEAT + EXTRA, TOK)]
    return call(normed_kernel, "normed_blocks", 8, [IN_VMEM] * 3, outs, [], 2 * TOK * D * WQ, (dproj_t, low_t, w))


def weight_send_kernel(low_t, grad_t, dproj, attended, out):
    for j in range(8):
        at = strip_of(j, 1)
        out[j, :, :WQ] = dot(low_t[at, :], dproj[...], NN).astype(BF16)
        out[j, :, WQ:] = dot(grad_t[at, :], attended[...], NN).astype(BF16)


def weight_keep_kernel(low_t, grad_t, dproj, attended, came, *outs):
    half = ROWS // 2
    for j in range(8):
        at = strip_of(j, 0)
        first = dot(low_t[at, :], dproj[...], NN) + came[j, :, :WQ].astype(F32)
        second = dot(grad_t[at, :], attended[...], NN) + came[j, :, WQ:].astype(F32)
        block = jnp.concatenate([first.astype(BF16), second.astype(BF16)], axis=1)
        if j < 2:
            outs[2 * j][...] = block[:half]
            outs[2 * j + 1][...] = block[half:]
        else:
            outs[j + 2][...] = block


def weight_blocks(low_t, grad_t, dproj, attended, came=None):
    args = (low_t, grad_t, dproj, attended)
    if came is None:
        kernel, name, outs = weight_send_kernel, "weight_send", [either((8, ROWS, WALL))]
    else:
        shapes = [(ROWS // 2, WALL)] * 4 + [(ROWS, WALL)] * 6
        kernel, name, outs = weight_keep_kernel, "weight_keep", [either(s) for s in shapes]
        args = args + (came,)
    return call(kernel, name, 8, [IN_VMEM] * len(args), outs, [], TOK * D * WALL, args)


def plus(*values):
    return functools.reduce(lambda a, b: a + b, [v.astype(F32) for v in values]).astype(BF16)


def grads_kernel(a, b, c, d, out_in, out_out):
    total = a[...].astype(F32) + b[...].astype(F32) + c[...].astype(F32) + d[...].astype(F32)
    out_in[...] = total[:, :WQ]
    out_out[...] = total[:, WQ:]


def last_grads(parts):
    outs = [either((ROWS, WQ), F32), either((ROWS, WA), F32)]
    return call(grads_kernel, "last_grads", 8, [IN_VMEM] * 4, outs, [], 4 * ROWS * WALL, parts)


def update_kernel(a, b, c, d, out):
    total = a[...].astype(F32) + b[...].astype(F32) + c[...].astype(F32) + d[...].astype(F32)
    out[...] = total.T.astype(BF16)


def last_update(parts):
    return call(update_kernel, "last_update", 8, [IN_VMEM] * 4, [either((TOK, FEAT))], [], TOK * FEAT, parts)[0]


def input_kernel(a, b, c, d, tokens, mean, inv, out):
    total = a[...].astype(F32) + b[...].astype(F32) + c[...].astype(F32) + d[...].astype(F32)
    value = (total[:FEAT] - total[FEAT : FEAT + 1] * (1.0 / D)).T
    cross = jnp.broadcast_to(total[FEAT + 1 : FEAT + 2] * (1.0 / D), (8, TOK)).T[:, :1]
    i = inv[...]
    normed = (tokens[...].astype(F32) - mean[...]) * i
    out[...] = (i * (value - normed * cross)).astype(BF16)


def last_input(parts, tokens, mean, inv):
    args = (*parts, tokens, mean, inv)
    return call(input_kernel, "last_input", 8, [IN_VMEM] * 7, [either((TOK, FEAT))], [], TOK * FEAT, args)[0]


def local(tokens, update_grad, weight_in, weight_out):
    half, r = TOK // 2, ROWS // 2
    own = jnp.concatenate([weight_in, weight_out], axis=1)
    t_ap, t_am = y_up(tokens), y_down(tokens)
    w_xx = x_near(own)
    w_up, w_down = z_up(own), z_down(own)

    g_own = after(update_grad, t_ap, t_am)
    g_ap, g_am = y_up(g_own), y_down(g_own)
    t_own = after(tokens, g_own, w_xx)
    t_xx = x_far(t_own)
    w_xx = after(w_xx, t_own, w_up, w_down)
    w_bp, w_bm = z_up(w_xx), z_down(w_xx)
    g_own = after(update_grad, w_xx, g_ap, g_am)
    g_xx = x_far(g_own)
    t_xx = after(t_xx, g_own)
    t_bp, t_bm = y_up(t_xx), y_down(t_xx)
    w_bp, w_bm = after((w_bp, w_bm), t_xx)
    w_s0, w_s1 = jnp.stack([w_up[:r], w_bp[:r]]), jnp.stack([w_down[r:], w_bm[r:]])
    w_f0, w_f1 = z_up(w_s0), z_down(w_s1)
    t_bp, t_bm = after((t_bp, t_bm), w_s0, w_s1)
    t_s0, t_s1 = jnp.stack([t_ap[:half], t_bp[:half]]), jnp.stack([t_am[half:], t_bm[half:]])
    t_f0, t_f1 = y_up(t_s0), y_down(t_s1)
    g_xx = after(g_xx, t_s0, t_s1)
    g_bp, g_bm = y_up(g_xx), y_down(g_xx)
    w_f0, w_f1 = after((w_f0, w_f1), g_xx)

    w_f0, w_f1 = after((w_f0, w_f1), t_f0, t_f1)
    mine = rows_in_order((own, w_xx, w_up, w_down, w_bp, w_bm, w_f0, w_f1))
    others = other_core(mine)
    t_f0, t_f1 = after((t_f0, t_f1), mine)
    low, low_t, mean, inv = tokens_in_order((tokens, t_ap, t_am, t_xx, t_bp, t_bm, t_f0, t_f1))
    g_bp, g_bm = after((g_bp, g_bm), low)
    g_s0, g_s1 = jnp.stack([g_ap[:half], g_bp[:half]]), jnp.stack([g_am[half:], g_bm[half:]])
    g_f0, g_f1 = y_up(g_s0), y_down(g_s1)

    (attended, proj, att, w), u = attend(after(low, g_s0, g_s1), mine, others)
    g_f0, g_f1 = after((g_f0, g_f1), attended)
    grad, grad_t = grad_in_order((update_grad, g_ap, g_am, g_xx, g_bp, g_bm, g_f0, g_f1))

    u_up, u_down = y_up(u[0]), y_down(u[1])
    dproj, dproj_t = attend_back(grad, w, proj, att)
    (send,) = weight_blocks(low_t, grad_t, dproj, attended)
    u_up, u_down = after((u_up, u_down), send)
    came = other_core(after(send, u_up, u_down))

    h = FEAT // 2
    u_s1 = jnp.stack([u[2].at[:h].set(plus(u[2][:h], u_up[0])), u[4].at[:h].set(plus(u[4][:h], u_up[1]))])
    u_s3 = jnp.stack([u[3].at[h:].set(plus(u[3][h:], u_down[0])), u[5].at[h:].set(plus(u[5][h:], u_down[1]))])
    u_r1, u_r3 = y_up(u_s1), y_down(u_s3)

    n = normed_blocks(after(dproj_t, u_s1, u_s3), low_t, w)
    keep = weight_blocks(low_t, grad_t, dproj, attended, after(came, n[7]))
    ka_up, ka_down = z_up(keep[0]), z_down(keep[1])

    u_r1, u_r3 = after((u_r1, u_r3), keep[9])
    u_x = x_far(plus(u[6], u_r1[0], u_r3[0]))
    n_first = after((n[0], n[1]), u_r1, u_r3)
    n_up, n_down = y_up(n_first[0]), y_down(n_first[1])

    ka_up, ka_down = after((ka_up, ka_down), *n_first)
    k_a = [keep[4].at[:r].set(plus(keep[4][:r], ka_up)), keep[5].at[r:].set(plus(keep[5][r:], ka_down))]
    k_r = z_up(k_a[0]), z_down(k_a[1])

    q = (FEAT + EXTRA) // 2
    n_up, n_down = after((n_up, n_down), *k_a)
    n_a = [n[2].at[:q].set(plus(n[2][:q], n_up[0])), n[3].at[q:].set(plus(n[3][q:], n_down[0]))]
    n_b = [n[4].at[:q].set(plus(n[4][:q], n_up[1])), n[5].at[q:].set(plus(n[5][q:], n_down[1]))]
    n_r = y_up(n_a[0]), y_down(n_a[1])

    k_r = after(k_r, u_x, *n_a)
    kb_first = after((keep[2], keep[3]), *k_r)
    kb_up, kb_down = z_up(kb_first[0]), z_down(kb_first[1])
    k_x = x_near(plus(keep[8], *k_r))
    k_b = [keep[6].at[:r].set(plus(keep[6][:r], kb_up)), keep[7].at[r:].set(plus(keep[7][r:], kb_down))]
    k_q = z_up(k_b[0]), z_down(k_b[1])

    n_r = after(n_r, *k_b)
    n_b = after(n_b, *n_r)
    n_q = y_up(n_b[0]), y_down(n_b[1])
    k_x = after(k_x, *n_b)
    n_x = x_far(after(plus(n[6], *n_r), k_x))

    update = last_update((u[7], u_r1[1], u_r3[1], u_x))
    weight_in_grad, weight_out_grad = last_grads((keep[9], *k_q, k_x))
    n_q, n_x = after((n_q, n_x), weight_in_grad)
    input_grad = last_input((n[7], *n_q, n_x), tokens, mean, inv)
    return (update, input_grad, weight_in_grad, weight_out_grad)


def solution(mesh):
    return jax.shard_map(
        local,
        mesh=mesh,
        in_specs=(P("dp", "mp"), P("dp", "mp"), P("dp", "mp"), P("dp", "mp")),
        out_specs=(P("dp", "mp"), P("dp", "mp"), P("dp", "mp"), P("dp", "mp")),
        check_vma=False,
    )
```

```python
import functools

import jax
import jax.numpy as jnp
from jax import lax
from jax.experimental import pallas as pl
from jax.experimental.pallas import tpu as pltpu
from jax.sharding import PartitionSpec as P

F32 = jnp.float32
BF16 = jnp.bfloat16

D = 3072
HD = 128
PATCH = 256
TOK = 512
HEADS = 3
WQ = HEADS * 3 * HD
WA = HEADS * HD
WALL = WQ + WA
FEAT = 384
ROWS = 192
EPS = 1e-06
EXTRA = 32

NN = (((1,), (0,)), ((), ()))
NT = (((1,), (1,)), ((), ()))
TN = (((0,), (0,)), ((), ()))

PIECES = ((0, 0), (0, 3), (0, 1), (0, 2), (1, 0), (1, 3), (1, 1), (1, 2))
BLOCKS = ((1, 2), (0, 2), (1, 1), (1, 3), (0, 1), (0, 3), (1, 0), (0, 0))


def dot(a, b, dims):
    return lax.dot_general(a, b, dims, preferred_element_type=F32)


def mp_perm(dx, dy):
    return [(x * 4 + y, ((x + dx) % 2) * 4 + (y + dy) % 4) for x in range(2) for y in range(4)]


def dp_perm(dz, dx, dc):
    return [
        ((z * 2 + x) * 2 + c, (((z + dz) % 4) * 2 + (x + dx) % 2) * 2 + (c + dc) % 2)
        for z in range(4)
        for x in range(2)
        for c in range(2)
    ]


def y_up(v):
    return lax.ppermute(v, "mp", mp_perm(0, 1))


def y_down(v):
    return lax.ppermute(v, "mp", mp_perm(0, 3))


def x_far(v):
    return lax.ppermute(v, "mp", mp_perm(1, 0))


def z_up(v):
    return lax.ppermute(v, "dp", dp_perm(1, 0, 0))


def z_down(v):
    return lax.ppermute(v, "dp", dp_perm(3, 0, 0))


def x_near(v):
    return lax.ppermute(v, "dp", dp_perm(0, 1, 0))


def other_core(v):
    return lax.ppermute(v, "dp", dp_perm(0, 0, 1))


IN_HBM = pl.BlockSpec(memory_space=pltpu.HBM)
IN_VMEM = pl.BlockSpec(memory_space=pltpu.VMEM)


def in_hbm(values):
    return [pltpu.with_memory_space_constraint(v, pltpu.HBM) for v in values]


def call(kernel, name, mib, ins, outs, scratch, flops, args):
    return pl.pallas_call(
        kernel,
        in_specs=ins,
        out_specs=[o for o, _ in outs],
        out_shape=[s for _, s in outs],
        scratch_shapes=scratch,
        compiler_params=pltpu.CompilerParams(vmem_limit_bytes=mib * 1024 * 1024),
        cost_estimate=pl.CostEstimate(flops=1024, bytes_accessed=1024, transcendentals=0),
        name=name,
    )(*args)


def to_vmem(shape, dtype=BF16):
    return IN_VMEM, pltpu.VMEM(shape, dtype)


def either(shape, dtype=BF16):
    return IN_VMEM, jax.ShapeDtypeStruct(shape, dtype)


def after(value, *others):
    return lax.optimization_barrier((value, others))[0]


def norm_rows(v):
    centred = v - jnp.mean(v, axis=-1, keepdims=True)
    inverse = lax.rsqrt(jnp.mean(centred * centred, axis=-1, keepdims=True) + EPS)
    return centred * inverse, inverse


def norm_back(incoming, normed, inverse):
    mean_in = jnp.mean(incoming, axis=-1, keepdims=True)
    mean_cross = jnp.mean(incoming * normed, axis=-1, keepdims=True)
    return inverse * (incoming - mean_in - normed * mean_cross)


PIECE_SHAPES = [(TOK, FEAT)] * 6 + [(2, TOK // 2, FEAT)] * 2


def piece_of(refs, k, at, rows):
    own, ap, am, xx, bp, bm, f0, f1 = refs
    if k == 3 or k == 7:
        half = TOK // 2
        return (f0 if at < half else f1)[k // 4, at % half : at % half + rows, :]
    return (own, ap, am, None, xx, bp, bm)[k][at : at + rows, :]


def columns_of(orders, k):
    m = lax.axis_index("mp")
    far, step = orders[k]
    owner = ((m // 4 + far) % 2) * 4 + (m + step) % 4
    return pl.ds(pl.multiple_of(owner * FEAT, FEAT), FEAT)


def strip_of(k, other):
    d = lax.axis_index("dp")
    far, step = BLOCKS[k]
    owner = ((d // 4 + step) % 4) * 4 + (((d // 2) + far) % 2) * 2 + (d + other) % 2
    return pl.ds(pl.multiple_of(owner * ROWS, ROWS), ROWS)


def tokens_kernel(*refs):
    held, (low, low_t, mean, inv) = refs[:8], refs[8:12]
    for at in range(0, TOK, HD):
        rows = slice(at, at + HD)
        total = jnp.zeros((HD, FEAT), F32)
        for k in range(8):
            total = total + piece_of(held, k, at, HD).astype(F32)
        m = jnp.sum(total, axis=-1, keepdims=True) * (1.0 / D)
        total = jnp.zeros((HD, FEAT), F32)
        for k in range(8):
            c = piece_of(held, k, at, HD).astype(F32) - m
            total = total + c * c
        i = lax.rsqrt(jnp.sum(total, axis=-1, keepdims=True) * (1.0 / D) + EPS)
        mean[rows, :] = m
        inv[rows, :] = i
        for k in range(8):
            to = columns_of(PIECES, k)
            n = ((piece_of(held, k, at, HD).astype(F32) - m) * i).astype(BF16)
            low[rows, to] = n
            low_t[to, rows] = n.T


def grad_kernel(*refs):
    held, (grad, grad_t) = refs[:8], refs[8:10]
    half = TOK // 2
    for k in range(8):
        to = columns_of(PIECES, k)
        for at in (0, half):
            v = piece_of(held, k, at, half)
            grad[at : at + half, to] = v
            grad_t[to, at : at + half] = v.T


def tokens_in_order(pieces):
    outs = [either((TOK, D)), either((D, TOK)), either((TOK, 1), F32), either((TOK, 1), F32)]
    return call(tokens_kernel, "tokens", 8, [IN_VMEM] * 8, outs, [], 20 * TOK * D, pieces)


def grad_in_order(pieces):
    outs = [either((TOK, D)), either((D, TOK))]
    return call(grad_kernel, "cotangent", 8, [IN_VMEM] * 8, outs, [], 2 * TOK * D, pieces)


def strips_kernel(*refs):
    for j, ref in enumerate(refs[:6]):
        refs[6][j] = ref[...]


def strips_together(pieces):
    return call(strips_kernel, "strips", 4, [IN_VMEM] * 6, [either((6, ROWS, WALL))], [], TOK, pieces)[0]


SCALE = HD**-0.5
UNITS = [(b, h) for b in range(TOK // PATCH) for h in range(HEADS)]


def head_part(ref, unit, p):
    b, h = unit
    c = (h * 3 + p) * HD
    return ref[b * PATCH : (b + 1) * PATCH, c : c + HD]


def attend_kernel(low, own, down, up, near, near_down, near_up, f0, f1, others, o_f0, o_f1, attended, proj, att, w, *outs):
    d = lax.axis_index("dp")
    half = ROWS // 2
    mine = (own, down, up, near, near_down, near_up)
    for step in range(4):
        z = (d // 4 + step) % 4
        for far in range(2):
            for other in range(2):
                strip = (z * 2 + (d // 2 + far) % 2) * 2 + (d + other) % 2
                to = pl.multiple_of(strip * ROWS, ROWS)
                if step == 2:
                    for i, ref in enumerate((o_f0, o_f1) if other else (f0, f1)):
                        w[pl.ds(pl.multiple_of(to + i * half, half), half), :] = ref[far]
                else:
                    j = far * 3 + (0, 1, None, 2)[step]
                    w[pl.ds(to, ROWS), :] = others[j] if other else mine[j][...]
        at = pl.ds(pl.multiple_of(z * 4 * ROWS, 4 * ROWS), 4 * ROWS)
        term = dot(low[:, at], w[at, :WQ], NN)
        if step == 0:
            proj[...] = term
        else:
            proj[...] += term
    ql = [norm_rows(head_part(proj, u, 0))[0].astype(BF16) for u in UNITS]
    kl = [norm_rows(head_part(proj, u, 1))[0].astype(BF16) for u in UNITS]
    vl = [head_part(proj, u, 2).astype(BF16) for u in UNITS]
    expo = [jnp.exp(dot(a, b, NT) * SCALE) for a, b in zip(ql, kl)]
    full = [v / jnp.sum(v, axis=-1, keepdims=True) for v in expo]
    mixed = [dot(a.astype(BF16), v, NN).astype(BF16) for a, v in zip(full, vl)]
    for i, (b, h) in enumerate(UNITS):
        att[i] = full[i]
        attended[b * PATCH : (b + 1) * PATCH, h * HD : (h + 1) * HD] = mixed[i]
    attended_t = attended[...].T
    for j in range(8):
        store_step(j, dot(w[columns_of(BLOCKS, j), WQ:], attended_t, NN).astype(BF16), outs)


def attend(low, *strips):
    outs = [either((TOK, WA)), to_vmem((TOK, WQ), F32), to_vmem((len(UNITS), PATCH, PATCH), F32), to_vmem((D, WALL))]
    outs += [either(s) for s in step_shapes(FEAT, TOK)]
    flops = 2 * TOK * D * WALL + 4 * TOK * PATCH * WA
    out = call(attend_kernel, "attend", 12, [IN_VMEM] * 12, outs, [], flops, (low, *strips))
    return out[:4], out[4:]


def back_kernel(grad, w, proj, att, dproj, dproj_t):
    ag = dot(grad[...], w[:, WQ:], NN).astype(BF16)

    def keep(unit, p, value):
        b, h = unit
        c = (h * 3 + p) * HD
        value = value.astype(BF16)
        dproj[b * PATCH : (b + 1) * PATCH, c : c + HD] = value
        dproj_t[c : c + HD, b * PATCH : (b + 1) * PATCH] = value.T

    queries = [norm_rows(head_part(proj, u, 0)) for u in UNITS]
    keys = [norm_rows(head_part(proj, u, 1)) for u in UNITS]
    ql = [v[0].astype(BF16) for v in queries]
    kl = [v[0].astype(BF16) for v in keys]
    vl = [head_part(proj, u, 2).astype(BF16) for u in UNITS]
    gl = [ag[b * PATCH : (b + 1) * PATCH, h * HD : (h + 1) * HD] for b, h in UNITS]
    mixes = [dot(g, v, NT) for g, v in zip(gl, vl)]
    sg = [att[i] * (m - jnp.sum(m * att[i], axis=-1, keepdims=True)) for i, m in enumerate(mixes)]
    sg = [(v * SCALE).astype(BF16) for v in sg]
    for i, u in enumerate(UNITS):
        keep(u, 2, dot(att[i].astype(BF16), gl[i], TN))
    for u, v, k, q in zip(UNITS, sg, kl, queries):
        keep(u, 0, norm_back(dot(v, k, NN), *q))
    for u, v, q, k in zip(UNITS, sg, ql, keys):
        keep(u, 1, norm_back(dot(v, q, TN), *k))


def attend_back(grad, w, proj, att):
    outs = [either((TOK, WQ)), either((WQ, TOK))]
    flops = 2 * TOK * D * WA + 8 * TOK * PATCH * WA
    return call(back_kernel, "attend_back", 16, [IN_VMEM] * 4, outs, [], flops, (grad, w, proj, att))


def store_step(j, block, outs):
    half = block.shape[0] // 2
    if j < 2:
        outs[0][j] = block[:half]
        outs[1][j] = block[half:]
    else:
        outs[j][...] = block


def step_shapes(rows, width):
    return [(2, rows // 2, width)] * 2 + [(rows, width)] * 6


def normed_kernel(dproj_t, low_t, w, *outs):
    half = (FEAT + EXTRA) // 2
    s_in = jnp.zeros((1, TOK), F32)
    s_cross = jnp.zeros((1, TOK), F32)
    for j in range(8):
        at = columns_of(BLOCKS, j)
        block = dot(w[at, :WQ], dproj_t[...], NN)
        s_in = s_in + jnp.sum(block, axis=0, keepdims=True)
        s_cross = s_cross + jnp.sum(block * low_t[at, :].astype(F32), axis=0, keepdims=True)
        block = block.astype(BF16)
        if j < 2:
            outs[0][j] = block[:half]
            outs[1][j, : FEAT - half] = block[half:]
        else:
            outs[j][:FEAT] = block
    stats = jnp.concatenate([s_in, s_cross, jnp.zeros((EXTRA - 2, TOK), F32)], axis=0).astype(BF16)
    for j in range(8):
        if j < 2:
            outs[1][j, FEAT - half :] = stats
        else:
            outs[j][FEAT:] = stats


def normed_blocks(dproj_t, low_t, w):
    outs = [either(s) for s in step_shapes(FEAT + EXTRA, TOK)]
    return call(normed_kernel, "normed_blocks", 8, [IN_VMEM] * 3, outs, [], 2 * TOK * D * WQ, (dproj_t, low_t, w))


def weight_send_kernel(low_t, grad_t, dproj, attended, out):
    for j in range(8):
        at = strip_of(j, 1)
        out[j, :, :WQ] = dot(low_t[at, :], dproj[...], NN).astype(BF16)
        out[j, :, WQ:] = dot(grad_t[at, :], attended[...], NN).astype(BF16)


def weight_keep_kernel(low_t, grad_t, dproj, attended, came, *outs):
    half = ROWS // 2
    for j in range(8):
        at = strip_of(j, 0)
        first = dot(low_t[at, :], dproj[...], NN) + came[j, :, :WQ].astype(F32)
        second = dot(grad_t[at, :], attended[...], NN) + came[j, :, WQ:].astype(F32)
        block = jnp.concatenate([first.astype(BF16), second.astype(BF16)], axis=1)
        if j < 2:
            outs[2 * j][...] = block[:half]
            outs[2 * j + 1][...] = block[half:]
        else:
            outs[j + 2][...] = block


def weight_blocks(low_t, grad_t, dproj, attended, came=None):
    args = (low_t, grad_t, dproj, attended)
    if came is None:
        kernel, name, outs = weight_send_kernel, "weight_send", [either((8, ROWS, WALL))]
    else:
        shapes = [(ROWS // 2, WALL)] * 4 + [(ROWS, WALL)] * 6
        kernel, name, outs = weight_keep_kernel, "weight_keep", [either(s) for s in shapes]
        args = args + (came,)
    return call(kernel, name, 8, [IN_VMEM] * len(args), outs, [], TOK * D * WALL, args)


def plus(*values):
    return functools.reduce(lambda a, b: a + b, [v.astype(F32) for v in values]).astype(BF16)


def grads_kernel(a, b, c, d, out_in, out_out):
    total = a[...].astype(F32) + b[...].astype(F32) + c[...].astype(F32) + d[...].astype(F32)
    out_in[...] = total[:, :WQ]
    out_out[...] = total[:, WQ:]


def last_grads(parts):
    outs = [either((ROWS, WQ), F32), either((ROWS, WA), F32)]
    return call(grads_kernel, "last_grads", 8, [IN_VMEM] * 4, outs, [], 4 * ROWS * WALL, parts)


def update_kernel(a, b, c, d, out):
    total = a[...].astype(F32) + b[...].astype(F32) + c[...].astype(F32) + d[...].astype(F32)
    out[...] = total.T.astype(BF16)


def last_update(parts):
    return call(update_kernel, "last_update", 8, [IN_VMEM] * 4, [either((TOK, FEAT))], [], TOK * FEAT, parts)[0]


def input_kernel(a, b, c, d, tokens, mean, inv, out):
    total = a[...].astype(F32) + b[...].astype(F32) + c[...].astype(F32) + d[...].astype(F32)
    value = (total[:FEAT] - total[FEAT : FEAT + 1] * (1.0 / D)).T
    cross = jnp.broadcast_to(total[FEAT + 1 : FEAT + 2] * (1.0 / D), (8, TOK)).T[:, :1]
    i = inv[...]
    normed = (tokens[...].astype(F32) - mean[...]) * i
    out[...] = (i * (value - normed * cross)).astype(BF16)


def last_input(parts, tokens, mean, inv):
    args = (*parts, tokens, mean, inv)
    return call(input_kernel, "last_input", 8, [IN_VMEM] * 7, [either((TOK, FEAT))], [], TOK * FEAT, args)[0]


def local(tokens, update_grad, weight_in, weight_out):
    half, r = TOK // 2, ROWS // 2
    t_xx = x_far(tokens)
    own = jnp.concatenate([weight_in, weight_out], axis=1)
    w_xx = x_near(own)
    t_own = after(tokens, own)
    t_ap, t_am = y_up(t_own), y_down(t_own)
    w_up, w_down = z_up(own), z_down(own)

    g_own = after(update_grad, t_ap, t_am, t_xx)
    g_ap, g_am = y_up(g_own), y_down(g_own)

    t_xx = after(t_xx, g_own, w_up, w_down)
    t_bp, t_bm = y_up(t_xx), y_down(t_xx)
    w_xx = after(w_xx, t_xx, g_ap, g_am)
    w_bp, w_bm = z_up(w_xx), z_down(w_xx)
    g_xx = x_far(after(update_grad, w_xx))

    t_bp, t_bm = after((t_bp, t_bm), w_xx)
    t_s0, t_s1 = jnp.stack([t_ap[:half], t_bp[:half]]), jnp.stack([t_am[half:], t_bm[half:]])
    t_f0, t_f1 = y_up(t_s0), y_down(t_s1)

    w_bp, w_bm = after((w_bp, w_bm), t_s0, t_s1)
    w_s0, w_s1 = jnp.stack([w_up[:r], w_bp[:r]]), jnp.stack([w_down[r:], w_bm[r:]])
    w_f0, w_f1 = z_up(w_s0), z_down(w_s1)

    t_f0, t_f1, g_xx = after((t_f0, t_f1, g_xx), w_s0, w_s1)
    g_xx = after(g_xx, t_f0, t_f1)
    g_bp, g_bm = y_up(g_xx), y_down(g_xx)
    others = other_core(strips_together((own, w_down, w_up, w_xx, w_bm, after(w_bp, g_xx))))
    low, low_t, mean, inv = tokens_in_order((tokens, t_ap, t_am, t_xx, t_bp, t_bm, after(t_f0, g_xx), t_f1))

    w_f0, w_f1, others = after((w_f0, w_f1, others), low)
    g_bp, g_bm = after((g_bp, g_bm), w_f0, w_f1, others)
    w_f0, w_f1 = after((w_f0, w_f1), g_bp, g_bm)
    o_f0, o_f1 = other_core(w_f0), other_core(w_f1)
    g_s0, g_s1 = jnp.stack([g_ap[:half], g_bp[:half]]), jnp.stack([g_am[half:], g_bm[half:]])
    g_f0, g_f1 = y_up(g_s0), y_down(g_s1)

    low = after(low, g_s0, g_s1)
    strips = (own, w_down, w_up, w_xx, w_bm, w_bp, w_f0, w_f1, others, o_f0, o_f1)
    (attended, proj, att, w), u = attend(low, *strips)
    g_f0, g_f1 = after((g_f0, g_f1), attended)
    grad, grad_t = grad_in_order((update_grad, g_ap, g_am, g_xx, g_bp, g_bm, g_f0, g_f1))

    u_up, u_down = y_up(u[0]), y_down(u[1])
    dproj, dproj_t = attend_back(grad, w, proj, att)
    (send,) = weight_blocks(low_t, grad_t, dproj, attended)
    u_up, u_down = after((u_up, u_down), send)
    came = other_core(after(send, u_up, u_down))

    h = FEAT // 2
    u_s1 = jnp.stack([u[2].at[:h].set(plus(u[2][:h], u_up[0])), u[4].at[:h].set(plus(u[4][:h], u_up[1]))])
    u_s3 = jnp.stack([u[3].at[h:].set(plus(u[3][h:], u_down[0])), u[5].at[h:].set(plus(u[5][h:], u_down[1]))])
    u_r1, u_r3 = y_up(u_s1), y_down(u_s3)

    n = normed_blocks(after(dproj_t, u_s1, u_s3), low_t, w)
    keep = weight_blocks(low_t, grad_t, dproj, attended, after(came, n[7]))
    ka_up, ka_down = z_up(keep[0]), z_down(keep[1])

    u_r1, u_r3 = after((u_r1, u_r3), keep[9])
    u_x = x_far(plus(u[6], u_r1[0], u_r3[0]))
    n_first = after((n[0], n[1]), u_r1, u_r3)
    n_up, n_down = y_up(n_first[0]), y_down(n_first[1])

    ka_up, ka_down = after((ka_up, ka_down), *n_first)
    k_a = [keep[4].at[:r].set(plus(keep[4][:r], ka_up)), keep[5].at[r:].set(plus(keep[5][r:], ka_down))]
    k_r = z_up(k_a[0]), z_down(k_a[1])

    q = (FEAT + EXTRA) // 2
    n_up, n_down = after((n_up, n_down), *k_a)
    n_a = [n[2].at[:q].set(plus(n[2][:q], n_up[0])), n[3].at[q:].set(plus(n[3][q:], n_down[0]))]
    n_b = [n[4].at[:q].set(plus(n[4][:q], n_up[1])), n[5].at[q:].set(plus(n[5][q:], n_down[1]))]
    n_r = y_up(n_a[0]), y_down(n_a[1])

    k_r = after(k_r, u_x, *n_a)
    kb_first = after((keep[2], keep[3]), *k_r)
    kb_up, kb_down = z_up(kb_first[0]), z_down(kb_first[1])
    k_x = x_near(plus(keep[8], *k_r))
    k_b = [keep[6].at[:r].set(plus(keep[6][:r], kb_up)), keep[7].at[r:].set(plus(keep[7][r:], kb_down))]
    k_q = z_up(k_b[0]), z_down(k_b[1])

    n_r = after(n_r, *k_b)
    n_b = after(n_b, *n_r)
    n_q = y_up(n_b[0]), y_down(n_b[1])
    k_x = after(k_x, *n_b)
    n_x = x_far(after(plus(n[6], *n_r), k_x))

    update = last_update((u[7], u_r1[1], u_r3[1], u_x))
    weight_in_grad, weight_out_grad = last_grads((keep[9], *k_q, k_x))
    n_q, n_x = after((n_q, n_x), weight_in_grad)
    input_grad = last_input((n[7], *n_q, n_x), tokens, mean, inv)
    return (update, input_grad, weight_in_grad, weight_out_grad)


def solution(mesh):
    return jax.shard_map(
        local,
        mesh=mesh,
        in_specs=(P("dp", "mp"), P("dp", "mp"), P("dp", "mp"), P("dp", "mp")),
        out_specs=(P("dp", "mp"), P("dp", "mp"), P("dp", "mp"), P("dp", "mp")),
        check_vma=False,
    )
```

```python
import functools

import jax
import jax.numpy as jnp
from jax import lax
from jax.experimental import pallas as pl
from jax.experimental.pallas import tpu as pltpu
from jax.sharding import PartitionSpec as P

F32 = jnp.float32
BF16 = jnp.bfloat16

D = 3072
HD = 128
PATCH = 256
TOK = 512
HEADS = 3
WQ = HEADS * 3 * HD
WA = HEADS * HD
WALL = WQ + WA
FEAT = 384
ROWS = 192
EPS = 1e-06
EXTRA = 32

NN = (((1,), (0,)), ((), ()))
NT = (((1,), (1,)), ((), ()))
TN = (((0,), (0,)), ((), ()))

PIECES = ((0, 0), (0, 3), (0, 1), (0, 2), (1, 0), (1, 3), (1, 1), (1, 2))
BLOCKS = ((1, 2), (0, 2), (1, 1), (1, 3), (0, 1), (0, 3), (1, 0), (0, 0))


def dot(a, b, dims):
    return lax.dot_general(a, b, dims, preferred_element_type=F32)


def mp_perm(dx, dy):
    return [(x * 4 + y, ((x + dx) % 2) * 4 + (y + dy) % 4) for x in range(2) for y in range(4)]


def dp_perm(dz, dx, dc):
    return [
        ((z * 2 + x) * 2 + c, (((z + dz) % 4) * 2 + (x + dx) % 2) * 2 + (c + dc) % 2)
        for z in range(4)
        for x in range(2)
        for c in range(2)
    ]


def y_up(v):
    return lax.ppermute(v, "mp", mp_perm(0, 1))


def y_down(v):
    return lax.ppermute(v, "mp", mp_perm(0, 3))


def x_far(v):
    return lax.ppermute(v, "mp", mp_perm(1, 0))


def z_up(v):
    return lax.ppermute(v, "dp", dp_perm(1, 0, 0))


def z_down(v):
    return lax.ppermute(v, "dp", dp_perm(3, 0, 0))


def x_near(v):
    return lax.ppermute(v, "dp", dp_perm(0, 1, 0))


def other_core(v):
    return lax.ppermute(v, "dp", dp_perm(0, 0, 1))


IN_HBM = pl.BlockSpec(memory_space=pltpu.HBM)
IN_VMEM = pl.BlockSpec(memory_space=pltpu.VMEM)


def in_hbm(values):
    return [pltpu.with_memory_space_constraint(v, pltpu.HBM) for v in values]


def call(kernel, name, mib, ins, outs, scratch, flops, args):
    return pl.pallas_call(
        kernel,
        in_specs=ins,
        out_specs=[o for o, _ in outs],
        out_shape=[s for _, s in outs],
        scratch_shapes=scratch,
        compiler_params=pltpu.CompilerParams(vmem_limit_bytes=mib * 1024 * 1024),
        cost_estimate=pl.CostEstimate(flops=1024, bytes_accessed=1024, transcendentals=0),
        name=name,
    )(*args)


def to_vmem(shape, dtype=BF16):
    return IN_VMEM, pltpu.VMEM(shape, dtype)


def either(shape, dtype=BF16):
    return IN_VMEM, jax.ShapeDtypeStruct(shape, dtype)


def after(value, *others):
    return lax.optimization_barrier((value, others))[0]


def norm_rows(v):
    centred = v - jnp.mean(v, axis=-1, keepdims=True)
    inverse = lax.rsqrt(jnp.mean(centred * centred, axis=-1, keepdims=True) + EPS)
    return centred * inverse, inverse


def norm_back(incoming, normed, inverse):
    mean_in = jnp.mean(incoming, axis=-1, keepdims=True)
    mean_cross = jnp.mean(incoming * normed, axis=-1, keepdims=True)
    return inverse * (incoming - mean_in - normed * mean_cross)


PIECE_SHAPES = [(TOK, FEAT)] * 6 + [(2, TOK // 2, FEAT)] * 2


def piece_of(refs, k, at, rows):
    own, ap, am, xx, bp, bm, f0, f1 = refs
    if k == 3 or k == 7:
        half = TOK // 2
        return (f0 if at < half else f1)[k // 4, at % half : at % half + rows, :]
    return (own, ap, am, None, xx, bp, bm)[k][at : at + rows, :]


def columns_of(orders, k):
    m = lax.axis_index("mp")
    far, step = orders[k]
    owner = ((m // 4 + far) % 2) * 4 + (m + step) % 4
    return pl.ds(pl.multiple_of(owner * FEAT, FEAT), FEAT)


def strip_of(k, other):
    d = lax.axis_index("dp")
    far, step = BLOCKS[k]
    owner = ((d // 4 + step) % 4) * 4 + (((d // 2) + far) % 2) * 2 + (d + other) % 2
    return pl.ds(pl.multiple_of(owner * ROWS, ROWS), ROWS)


def tokens_kernel(*refs):
    held, (low, low_t, mean, inv) = refs[:8], refs[8:12]
    for at in range(0, TOK, HD):
        rows = slice(at, at + HD)
        total = jnp.zeros((HD, FEAT), F32)
        for k in range(8):
            total = total + piece_of(held, k, at, HD).astype(F32)
        m = jnp.sum(total, axis=-1, keepdims=True) * (1.0 / D)
        total = jnp.zeros((HD, FEAT), F32)
        for k in range(8):
            c = piece_of(held, k, at, HD).astype(F32) - m
            total = total + c * c
        i = lax.rsqrt(jnp.sum(total, axis=-1, keepdims=True) * (1.0 / D) + EPS)
        mean[rows, :] = m
        inv[rows, :] = i
        for k in range(8):
            to = columns_of(PIECES, k)
            n = ((piece_of(held, k, at, HD).astype(F32) - m) * i).astype(BF16)
            low[rows, to] = n
            low_t[to, rows] = n.T


def grad_kernel(*refs):
    held, (grad, grad_t) = refs[:8], refs[8:10]
    half = TOK // 2
    for k in range(8):
        to = columns_of(PIECES, k)
        for at in (0, half):
            v = piece_of(held, k, at, half)
            grad[at : at + half, to] = v
            grad_t[to, at : at + half] = v.T


def tokens_in_order(pieces):
    outs = [either((TOK, D)), either((D, TOK)), either((TOK, 1), F32), either((TOK, 1), F32)]
    return call(tokens_kernel, "tokens", 8, [IN_VMEM] * 8, outs, [], 20 * TOK * D, pieces)


def grad_in_order(pieces):
    outs = [either((TOK, D)), either((D, TOK))]
    return call(grad_kernel, "cotangent", 8, [IN_VMEM] * 8, outs, [], 2 * TOK * D, pieces)


def strips_kernel(*refs):
    for j, ref in enumerate(refs[:6]):
        refs[6][j] = ref[...]


def strips_together(pieces):
    return call(strips_kernel, "strips", 4, [IN_VMEM] * 6, [either((6, ROWS, WALL))], [], TOK, pieces)[0]


SCALE = HD**-0.5
UNITS = [(b, h) for b in range(TOK // PATCH) for h in range(HEADS)]


def head_part(ref, unit, p):
    b, h = unit
    c = (h * 3 + p) * HD
    return ref[b * PATCH : (b + 1) * PATCH, c : c + HD]


def attend_kernel(low, own, down, up, near, near_down, near_up, f0, f1, others, o_f0, o_f1, attended, proj, att, w, *outs):
    d = lax.axis_index("dp")
    half = ROWS // 2
    mine = (own, down, up, near, near_down, near_up)
    for step in range(4):
        z = (d // 4 + step) % 4
        for far in range(2):
            for other in range(2):
                strip = (z * 2 + (d // 2 + far) % 2) * 2 + (d + other) % 2
                to = pl.multiple_of(strip * ROWS, ROWS)
                if step == 2:
                    for i, ref in enumerate((o_f0, o_f1) if other else (f0, f1)):
                        w[pl.ds(pl.multiple_of(to + i * half, half), half), :] = ref[far]
                else:
                    j = far * 3 + (0, 1, None, 2)[step]
                    w[pl.ds(to, ROWS), :] = others[j] if other else mine[j][...]
        at = pl.ds(pl.multiple_of(z * 4 * ROWS, 4 * ROWS), 4 * ROWS)
        term = dot(low[:, at], w[at, :WQ], NN)
        if step == 0:
            proj[...] = term
        else:
            proj[...] += term
    ql = [norm_rows(head_part(proj, u, 0))[0].astype(BF16) for u in UNITS]
    kl = [norm_rows(head_part(proj, u, 1))[0].astype(BF16) for u in UNITS]
    vl = [head_part(proj, u, 2).astype(BF16) for u in UNITS]
    expo = [jnp.exp(dot(a, b, NT) * SCALE) for a, b in zip(ql, kl)]
    full = [v / jnp.sum(v, axis=-1, keepdims=True) for v in expo]
    mixed = [dot(a.astype(BF16), v, NN).astype(BF16) for a, v in zip(full, vl)]
    for i, (b, h) in enumerate(UNITS):
        att[i] = full[i]
        attended[b * PATCH : (b + 1) * PATCH, h * HD : (h + 1) * HD] = mixed[i]
    attended_t = attended[...].T
    for j in range(8):
        store_step(j, dot(w[columns_of(BLOCKS, j), WQ:], attended_t, NN).astype(BF16), outs)


def attend(low, *strips):
    outs = [either((TOK, WA)), to_vmem((TOK, WQ), F32), to_vmem((len(UNITS), PATCH, PATCH), F32), to_vmem((D, WALL))]
    outs += [either(s) for s in step_shapes(FEAT, TOK)]
    flops = 2 * TOK * D * WALL + 4 * TOK * PATCH * WA
    out = call(attend_kernel, "attend", 12, [IN_VMEM] * 12, outs, [], flops, (low, *strips))
    return out[:4], out[4:]


def back_kernel(grad, w, proj, att, dproj, dproj_t):
    ag = dot(grad[...], w[:, WQ:], NN).astype(BF16)

    def keep(unit, p, value):
        b, h = unit
        c = (h * 3 + p) * HD
        value = value.astype(BF16)
        dproj[b * PATCH : (b + 1) * PATCH, c : c + HD] = value
        dproj_t[c : c + HD, b * PATCH : (b + 1) * PATCH] = value.T

    queries = [norm_rows(head_part(proj, u, 0)) for u in UNITS]
    keys = [norm_rows(head_part(proj, u, 1)) for u in UNITS]
    ql = [v[0].astype(BF16) for v in queries]
    kl = [v[0].astype(BF16) for v in keys]
    vl = [head_part(proj, u, 2).astype(BF16) for u in UNITS]
    gl = [ag[b * PATCH : (b + 1) * PATCH, h * HD : (h + 1) * HD] for b, h in UNITS]
    mixes = [dot(g, v, NT) for g, v in zip(gl, vl)]
    sg = [att[i] * (m - jnp.sum(m * att[i], axis=-1, keepdims=True)) for i, m in enumerate(mixes)]
    sg = [(v * SCALE).astype(BF16) for v in sg]
    for i, u in enumerate(UNITS):
        keep(u, 2, dot(att[i].astype(BF16), gl[i], TN))
    for u, v, k, q in zip(UNITS, sg, kl, queries):
        keep(u, 0, norm_back(dot(v, k, NN), *q))
    for u, v, q, k in zip(UNITS, sg, ql, keys):
        keep(u, 1, norm_back(dot(v, q, TN), *k))


def attend_back(grad, w, proj, att):
    outs = [either((TOK, WQ)), either((WQ, TOK))]
    flops = 2 * TOK * D * WA + 8 * TOK * PATCH * WA
    return call(back_kernel, "attend_back", 16, [IN_VMEM] * 4, outs, [], flops, (grad, w, proj, att))


def store_step(j, block, outs):
    half = block.shape[0] // 2
    if j < 2:
        outs[0][j] = block[:half]
        outs[1][j] = block[half:]
    else:
        outs[j][...] = block


def step_shapes(rows, width):
    return [(2, rows // 2, width)] * 2 + [(rows, width)] * 6


def normed_kernel(dproj_t, low_t, w, *outs):
    half = (FEAT + EXTRA) // 2
    s_in = jnp.zeros((1, TOK), F32)
    s_cross = jnp.zeros((1, TOK), F32)
    for j in range(8):
        at = columns_of(BLOCKS, j)
        block = dot(w[at, :WQ], dproj_t[...], NN)
        s_in = s_in + jnp.sum(block, axis=0, keepdims=True)
        s_cross = s_cross + jnp.sum(block * low_t[at, :].astype(F32), axis=0, keepdims=True)
        block = block.astype(BF16)
        if j < 2:
            outs[0][j] = block[:half]
            outs[1][j, : FEAT - half] = block[half:]
        else:
            outs[j][:FEAT] = block
    stats = jnp.concatenate([s_in, s_cross, jnp.zeros((EXTRA - 2, TOK), F32)], axis=0).astype(BF16)
    for j in range(8):
        if j < 2:
            outs[1][j, FEAT - half :] = stats
        else:
            outs[j][FEAT:] = stats


def normed_blocks(dproj_t, low_t, w):
    outs = [either(s) for s in step_shapes(FEAT + EXTRA, TOK)]
    return call(normed_kernel, "normed_blocks", 8, [IN_VMEM] * 3, outs, [], 2 * TOK * D * WQ, (dproj_t, low_t, w))


def weight_send_kernel(low_t, grad_t, dproj, attended, out):
    for j in range(8):
        at = strip_of(j, 1)
        out[j, :, :WQ] = dot(low_t[at, :], dproj[...], NN).astype(BF16)
        out[j, :, WQ:] = dot(grad_t[at, :], attended[...], NN).astype(BF16)


def weight_keep_kernel(low_t, grad_t, dproj, attended, came, *outs):
    half = ROWS // 2
    for j in range(8):
        at = strip_of(j, 0)
        first = dot(low_t[at, :], dproj[...], NN) + came[j, :, :WQ].astype(F32)
        second = dot(grad_t[at, :], attended[...], NN) + came[j, :, WQ:].astype(F32)
        block = jnp.concatenate([first.astype(BF16), second.astype(BF16)], axis=1)
        if j < 2:
            outs[2 * j][...] = block[:half]
            outs[2 * j + 1][...] = block[half:]
        else:
            outs[j + 2][...] = block


def weight_blocks(low_t, grad_t, dproj, attended, came=None):
    args = (low_t, grad_t, dproj, attended)
    if came is None:
        kernel, name, outs = weight_send_kernel, "weight_send", [either((8, ROWS, WALL))]
    else:
        shapes = [(ROWS // 2, WALL)] * 4 + [(ROWS, WALL)] * 6
        kernel, name, outs = weight_keep_kernel, "weight_keep", [either(s) for s in shapes]
        args = args + (came,)
    return call(kernel, name, 8, [IN_VMEM] * len(args), outs, [], TOK * D * WALL, args)


def plus(*values):
    return functools.reduce(lambda a, b: a + b, [v.astype(F32) for v in values]).astype(BF16)


def grads_kernel(a, b, c, d, out_in, out_out):
    total = a[...].astype(F32) + b[...].astype(F32) + c[...].astype(F32) + d[...].astype(F32)
    out_in[...] = total[:, :WQ]
    out_out[...] = total[:, WQ:]


def last_grads(parts):
    outs = [either((ROWS, WQ), F32), either((ROWS, WA), F32)]
    return call(grads_kernel, "last_grads", 8, [IN_VMEM] * 4, outs, [], 4 * ROWS * WALL, parts)


def update_kernel(a, b, c, d, out):
    total = a[...].astype(F32) + b[...].astype(F32) + c[...].astype(F32) + d[...].astype(F32)
    out[...] = total.T.astype(BF16)


def last_update(parts):
    return call(update_kernel, "last_update", 8, [IN_VMEM] * 4, [either((TOK, FEAT))], [], TOK * FEAT, parts)[0]


def input_kernel(a, b, c, d, tokens, mean, inv, out):
    total = a[...].astype(F32) + b[...].astype(F32) + c[...].astype(F32) + d[...].astype(F32)
    value = (total[:FEAT] - total[FEAT : FEAT + 1] * (1.0 / D)).T
    cross = jnp.broadcast_to(total[FEAT + 1 : FEAT + 2] * (1.0 / D), (8, TOK)).T[:, :1]
    i = inv[...]
    normed = (tokens[...].astype(F32) - mean[...]) * i
    out[...] = (i * (value - normed * cross)).astype(BF16)


def last_input(parts, tokens, mean, inv):
    args = (*parts, tokens, mean, inv)
    return call(input_kernel, "last_input", 8, [IN_VMEM] * 7, [either((TOK, FEAT))], [], TOK * FEAT, args)[0]


def local(tokens, update_grad, weight_in, weight_out):
    half, r = TOK // 2, ROWS // 2
    own = jnp.concatenate([weight_in, weight_out], axis=1)
    t_ap, t_am = y_up(tokens), y_down(tokens)
    w_xx = x_near(own)
    w_up, w_down = z_up(own), z_down(own)

    g_own = after(update_grad, t_ap, t_am)
    g_ap, g_am = y_up(g_own), y_down(g_own)
    t_own = after(tokens, g_own, w_xx)
    t_xx = x_far(t_own)
    w_xx = after(w_xx, t_own, w_up, w_down)
    w_bp, w_bm = z_up(w_xx), z_down(w_xx)
    g_own = after(update_grad, w_xx, g_ap, g_am)
    g_xx = x_far(g_own)
    t_xx = after(t_xx, g_own)
    t_bp, t_bm = y_up(t_xx), y_down(t_xx)
    w_bp, w_bm = after((w_bp, w_bm), t_xx)
    w_s0, w_s1 = jnp.stack([w_up[:r], w_bp[:r]]), jnp.stack([w_down[r:], w_bm[r:]])
    w_f0, w_f1 = z_up(w_s0), z_down(w_s1)
    t_bp, t_bm = after((t_bp, t_bm), w_s0, w_s1)
    t_s0, t_s1 = jnp.stack([t_ap[:half], t_bp[:half]]), jnp.stack([t_am[half:], t_bm[half:]])
    t_f0, t_f1 = y_up(t_s0), y_down(t_s1)
    g_xx = after(g_xx, t_s0, t_s1)
    g_bp, g_bm = y_up(g_xx), y_down(g_xx)
    others = other_core(strips_together((own, w_down, w_up, w_xx, w_bm, after(w_bp, g_xx))))
    low, low_t, mean, inv = tokens_in_order((tokens, t_ap, t_am, t_xx, t_bp, t_bm, after(t_f0, g_xx), t_f1))

    w_f0, w_f1, others = after((w_f0, w_f1, others), low)
    g_bp, g_bm = after((g_bp, g_bm), w_f0, w_f1, others)
    w_f0, w_f1 = after((w_f0, w_f1), g_bp, g_bm)
    o_f0, o_f1 = other_core(w_f0), other_core(w_f1)
    g_s0, g_s1 = jnp.stack([g_ap[:half], g_bp[:half]]), jnp.stack([g_am[half:], g_bm[half:]])
    g_f0, g_f1 = y_up(g_s0), y_down(g_s1)

    low = after(low, g_s0, g_s1)
    strips = (own, w_down, w_up, w_xx, w_bm, w_bp, w_f0, w_f1, others, o_f0, o_f1)
    (attended, proj, att, w), u = attend(low, *strips)
    g_f0, g_f1 = after((g_f0, g_f1), attended)
    grad, grad_t = grad_in_order((update_grad, g_ap, g_am, g_xx, g_bp, g_bm, g_f0, g_f1))

    u_up, u_down = y_up(u[0]), y_down(u[1])
    dproj, dproj_t = attend_back(grad, w, proj, att)
    (send,) = weight_blocks(low_t, grad_t, dproj, attended)
    u_up, u_down = after((u_up, u_down), send)
    came = other_core(after(send, u_up, u_down))

    h = FEAT // 2
    u_s1 = jnp.stack([u[2].at[:h].set(plus(u[2][:h], u_up[0])), u[4].at[:h].set(plus(u[4][:h], u_up[1]))])
    u_s3 = jnp.stack([u[3].at[h:].set(plus(u[3][h:], u_down[0])), u[5].at[h:].set(plus(u[5][h:], u_down[1]))])
    u_r1, u_r3 = y_up(u_s1), y_down(u_s3)

    n = normed_blocks(after(dproj_t, u_s1, u_s3), low_t, w)
    keep = weight_blocks(low_t, grad_t, dproj, attended, after(came, n[7]))
    ka_up, ka_down = z_up(keep[0]), z_down(keep[1])

    u_r1, u_r3 = after((u_r1, u_r3), keep[9])
    u_x = x_far(plus(u[6], u_r1[0], u_r3[0]))
    n_first = after((n[0], n[1]), u_r1, u_r3)
    n_up, n_down = y_up(n_first[0]), y_down(n_first[1])

    ka_up, ka_down = after((ka_up, ka_down), *n_first)
    k_a = [keep[4].at[:r].set(plus(keep[4][:r], ka_up)), keep[5].at[r:].set(plus(keep[5][r:], ka_down))]
    k_r = z_up(k_a[0]), z_down(k_a[1])

    q = (FEAT + EXTRA) // 2
    n_up, n_down = after((n_up, n_down), *k_a)
    n_a = [n[2].at[:q].set(plus(n[2][:q], n_up[0])), n[3].at[q:].set(plus(n[3][q:], n_down[0]))]
    n_b = [n[4].at[:q].set(plus(n[4][:q], n_up[1])), n[5].at[q:].set(plus(n[5][q:], n_down[1]))]
    n_r = y_up(n_a[0]), y_down(n_a[1])

    k_r = after(k_r, u_x, *n_a)
    kb_first = after((keep[2], keep[3]), *k_r)
    kb_up, kb_down = z_up(kb_first[0]), z_down(kb_first[1])
    k_x = x_near(plus(keep[8], *k_r))
    k_b = [keep[6].at[:r].set(plus(keep[6][:r], kb_up)), keep[7].at[r:].set(plus(keep[7][r:], kb_down))]
    k_q = z_up(k_b[0]), z_down(k_b[1])

    n_r = after(n_r, *k_b)
    n_b = after(n_b, *n_r)
    n_q = y_up(n_b[0]), y_down(n_b[1])
    k_x = after(k_x, *n_b)
    n_x = x_far(after(plus(n[6], *n_r), k_x))

    update = last_update((u[7], u_r1[1], u_r3[1], u_x))
    weight_in_grad, weight_out_grad = last_grads((keep[9], *k_q, k_x))
    n_q, n_x = after((n_q, n_x), weight_in_grad)
    input_grad = last_input((n[7], *n_q, n_x), tokens, mean, inv)
    return (update, input_grad, weight_in_grad, weight_out_grad)


def solution(mesh):
    return jax.shard_map(
        local,
        mesh=mesh,
        in_specs=(P("dp", "mp"), P("dp", "mp"), P("dp", "mp"), P("dp", "mp")),
        out_specs=(P("dp", "mp"), P("dp", "mp"), P("dp", "mp"), P("dp", "mp")),
        check_vma=False,
    )
```
